512 devices in a mesh: gx: 16 (over z_lo, core), gy: 16 (over y, x), gz: 2 (over z_hi).
Axes of the slice: x: 4, y: 4, z: 16 (z_hi: 2, z_lo: 8; z = z_hi * 8 + z_lo), core: 2. Of those that a mesh axis runs over, the one named last changes fastest.
Arguments:
- log_range: float32 [32, 512, 2048], P('gz', 'gx', 'gy'), may hold values from -0.5 to 1.5
- sea_mask: int32 [32, 512, 2048], P('gz', 'gx', 'gy'), may hold values 0 or 1
- forcing: float32 [32, 512, 2048], P('gz', 'gx', 'gy'), may hold values from -24 to 24
- cotangent: float32 [32, 512, 2048], P('gz', 'gx', 'gy'), may hold values from -24 to 24
Outputs:
- iterate: float32 [32, 512, 2048], P('gz', 'gx', 'gy')
- range_grad: float32 [32, 512, 2048], P('gz', 'gx', 'gy')
The draws below stay inside these ranges and needn't reach their ends.
All inputs are finite; a program needn't handle non-finite values. No bound on the sum of `sea_mask` on one device may be relied on, other than what follows from the above.
Results may differ from the reference program's by a relative error of at most 0.00002.
Values sent between devices are 32-bit elements; how exact they have to be, the bound alone decides.
A program may use at most 64 MiB of HBM per device.

```python
import jax
import jax.numpy as jnp

SWEEPS = 4
NZ = 32
NX = 512
NY = 2048


def plant(drawn, own_key, smallest, largest):
    longest = drawn.shape.index(max(drawn.shape))
    spots = []
    for shift in (0, 1):
        where = [jax.random.randint(jax.random.fold_in(own_key, axis), (), 0, length) for axis, length in enumerate(drawn.shape)]
        where[longest] = (where[longest] + shift) % drawn.shape[longest]
        spots.append(tuple(where))
    return drawn.at[spots[0]].set(smallest).at[spots[1]].set(largest)


def steps_of(key, dims, cuts, least, top_value):
    gain, own = 1.0, jax.random.fold_in(key, 6)
    for axis_at, parts in cuts:
        heights = jnp.exp(jax.random.uniform(jax.random.fold_in(own, axis_at), (parts,), jnp.float32, least / len(cuts), top_value / len(cuts)))
        gain = gain * jnp.repeat(heights, dims[axis_at] // parts).reshape([-1 if axis == axis_at else 1 for axis in range(len(dims))])
    return gain


def normal_values(own_key, shape, deviation, limit, shards=(), dtype=jnp.bfloat16):
    entries = deviation * jax.random.normal(own_key, shape, jnp.float32)
    if shards:
        entries = entries * steps_of(own_key, shape, shards, -0.22, 0.18)
    return jnp.clip(entries, -limit, limit).astype(dtype)


def setup_inputs(seed: int = 0) -> dict:
    arg_keys = jax.random.split(jax.random.key(seed), 5)
    return {
        "log_range": jnp.clip(-0.5 + 2.0 * jax.random.uniform(arg_keys[0], (NZ, NX, NY), jnp.float32) ** steps_of(arg_keys[0], (NZ, NX, NY), ((0, 2), (1, 16), (2, 16)), -0.2, 0.2), -0.5, 1.5),
        "sea_mask": plant((jax.random.randint(arg_keys[1], (NZ, NX, NY), 0, 4) < 3).astype(jnp.int32), jax.random.fold_in(arg_keys[1], 1), 0, 1),
        "forcing": normal_values(arg_keys[2], (NZ, NX, NY), 4.0, 24.0, ((0, 2), (1, 16), (2, 16)), jnp.float32),
        "cotangent": normal_values(arg_keys[3], (NZ, NX, NY), 4.0, 24.0, ((0, 2), (1, 16), (2, 16)), jnp.float32),
    }


relaxation = 0.9

def neighbours(field):
    padded = jnp.pad(field, 1)
    total = padded[2:, 1:-1, 1:-1] + padded[:-2, 1:-1, 1:-1]
    total = total + padded[1:-1, 2:, 1:-1] + padded[1:-1, :-2, 1:-1]
    total = total + padded[1:-1, 1:-1, 2:] + padded[1:-1, 1:-1, :-2]
    return total

def reference(log_range, sea_mask, forcing, cotangent):
    sea = sea_mask.astype(jnp.float32)

    def sweeps(values):
        diagonal = sea * (6.0 + jnp.exp(-2.0 * values)) + (1.0 - sea)
        state = jnp.zeros_like(forcing)
        for step in range(SWEEPS):
            state = (1.0 - relaxation) * state + relaxation * (forcing + sea * neighbours(sea * state)) / diagonal
        return state
    iterate, pullback = jax.vjp(sweeps, log_range)
    range_grad = pullback(cotangent)[0]
    return (iterate, range_grad)
```

```python
import functools

import jax
import jax.numpy as jnp
from jax import lax
from jax.experimental import pallas as pl
from jax.experimental.pallas import tpu as pltpu
from jax.sharding import PartitionSpec as P

MESH = pl.DeviceIdType.MESH
RELAX = 0.9
KEEP = 1.0 - RELAX
LAND = RELAX * (1.0 + KEEP + KEEP * KEEP + KEEP * KEEP * KEEP)
OWN = pl.ds(8, 32)


def roll(value, shift, axis):
    size = value.shape[axis]
    shift = shift % size
    return pltpu.roll(value, shift, axis) if shift else value


def stencil_full(ref, i):
    lane = lax.broadcasted_iota(jnp.int32, (48, 128), 1)
    first, last = lane == 0, lane == 127
    c0, c1 = ref[i, 0], ref[i, 1]
    r0, r1 = roll(c0, 1, 1), roll(c1, 1, 1)
    l0, l1 = roll(c0, -1, 1), roll(c1, -1, 1)
    n0 = ref[i - 1, 0] + ref[i + 1, 0] + (roll(c0, 1, 0) + roll(c0, -1, 0))
    n1 = ref[i - 1, 1] + ref[i + 1, 1] + (roll(c1, 1, 0) + roll(c1, -1, 0))
    n0 = n0 + jnp.where(first, r1, r0) + jnp.where(last, l1, l0)
    n1 = n1 + jnp.where(first, r0, r1) + jnp.where(last, l0, l1)
    return (c0, c1), (n0, n1)


def stencil_own(ref, i):
    lane = lax.broadcasted_iota(jnp.int32, (32, 128), 1)
    c = ref[i, 0]
    own = c[8:40]
    side = ref[i, 1, OWN]
    n = ref[i - 1, 0, OWN] + ref[i + 1, 0, OWN]
    n = n + (roll(c, 1, 0)[8:40] + roll(c, -1, 0)[8:40])
    n = n + jnp.where(lane == 0, roll(side, 1, 1), roll(own, 1, 1))
    n = n + jnp.where(lane == 127, roll(side, -1, 1), roll(own, -1, 1))
    return own, n


def kernel(sizes, lr_h, m_h, f_h, c_h, it_h, rg_h,
           lr, ms, fo, co, it, rg, a_, u1, u2, u3, w0, w1, w2,
           xs, xr, ys, yr, zs, zr, gs, gr, in_sem, out_sem, sem):
    nx, ny = sizes
    gz, gx, gy = lax.axis_index("gz"), lax.axis_index("gx"), lax.axis_index("gy")
    has = [gx > 0, gx < nx - 1, gy > 0, gy < ny - 1]
    to = [{"gx": gx - 1}, {"gx": gx + 1}, {"gy": gy - 1}, {"gy": gy + 1}]
    partner = {"gz": 1 - gz}

    barrier = pltpu.get_barrier_semaphore()
    pl.semaphore_signal(barrier, inc=1, device_id=partner, device_id_type=MESH)
    for here, device in zip(has, to):
        @pl.when(here)
        def _():
            pl.semaphore_signal(barrier, inc=1, device_id=device, device_id_type=MESH)

    loads = [pltpu.make_async_copy(h, v, in_sem.at[i]) for i, (h, v) in enumerate(((lr_h, lr), (m_h, ms), (f_h, fo), (c_h, co)))]
    for load in loads:
        load.start()

    def remote(src, dst, i, device):
        return pltpu.make_async_remote_copy(src_ref=src, dst_ref=dst, send_sem=sem.at[0, i], recv_sem=sem.at[1, i],
                                            device_id=device, device_id_type=MESH)

    xcopy = [remote(xs.at[0], xr.at[0], 0, to[0]), remote(xs.at[1], xr.at[1], 1, to[1])]
    ycopy = [remote(ys.at[0], yr.at[0], 2, to[2]), remote(ys.at[1], yr.at[1], 3, to[3])]
    zcopy = remote(zs, zr, 4, partner)
    gcopy = remote(gs, gr, 5, partner)

    def source(i):
        return jnp.where(gz == 0, i, 15 - i)

    row8 = lax.broadcasted_iota(jnp.int32, (8, 128), 0)
    lane8 = lax.broadcasted_iota(jnp.int32, (8, 128), 1)
    lane48 = lax.broadcasted_iota(jnp.int32, (48, 128), 1)
    zero = jnp.zeros((48, 128), jnp.float32)
    for ref in (u1, u2, u3, w0, w1, w2):
        ref[0, 0] = zero
        ref[0, 1] = zero
    for load in loads:
        load.wait()

    def prepare(i, _):
        z = source(i)
        mask = ms[z].astype(jnp.float32)
        inverse = 1.0 / (mask * (6.0 + jnp.exp(-2.0 * lr[z])) + (1.0 - mask))
        weight = RELAX * mask * inverse
        u, w = weight * fo[z], weight * co[z]
        a_[i + 1, 0, OWN] = weight
        u1[i + 1, 0, OWN] = u
        w0[i + 1, 0, OWN] = w
        up_u, up_w, up_a = u[:8], w[:8], weight[:8]
        dn_u, dn_w, dn_a = u[24:], w[24:], weight[24:]
        xs[0, i] = jnp.where(row8 < 3, up_u, jnp.where(row8 < 6, roll(up_w, 3, 0), roll(up_a, 6, 0)))
        xs[1, i] = jnp.where(row8 >= 5, dn_u, jnp.where(row8 >= 2, roll(dn_w, -3, 0), roll(dn_a, -6, 0)))
        return 0

    lax.fori_loop(0, 16, prepare, 0)
    for j in range(3):
        zs[j] = u1[16 - j, 0, OWN]
        zs[3 + j] = w0[16 - j, 0, OWN]
    for j in range(2):
        zs[6 + j] = a_[16 - j, 0, OWN]

    pl.semaphore_wait(barrier, 1 + sum(h.astype(jnp.int32) for h in has))
    for here, copy in zip(has[:2], xcopy):
        @pl.when(here)
        def _():
            copy.start()
    zcopy.start()

    for here, copy in zip((has[1], has[0]), xcopy):
        @pl.when(here)
        def _():
            copy.wait_recv()

    def x_halo(i, carry):
        right, left = carry
        low = jnp.where(has[1], xr[0, i], 0.0)
        top = jnp.where(has[0], xr[1, i], 0.0)
        u1[i + 1, 0, pl.ds(40, 8)] = low
        w0[i + 1, 0, pl.ds(40, 8)] = roll(low, -3, 0)
        a_[i + 1, 0, pl.ds(40, 8)] = roll(low, -6, 0)
        u1[i + 1, 0, pl.ds(0, 8)] = top
        w0[i + 1, 0, pl.ds(0, 8)] = roll(top, 3, 0)
        a_[i + 1, 0, pl.ds(0, 8)] = roll(top, 6, 0)
        u, w, weight = u1[i + 1, 0], w0[i + 1, 0], a_[i + 1, 0]
        to_right = jnp.where(lane48 < 3, roll(u, 3, 1), jnp.where(lane48 < 6, roll(w, 6, 1), roll(weight, 8, 1)))
        to_left = jnp.where(lane48 < 3, u, jnp.where(lane48 < 6, roll(w, 3, 1), roll(weight, 6, 1)))
        right = jnp.where(lane48 < 8, to_right, roll(right, 8, 1))
        left = jnp.where(lane48 < 8, to_left, roll(left, 8, 1))
        return right, left

    right, left = lax.fori_loop(0, 16, x_halo, (zero, zero))
    ys[1] = right
    ys[0] = left
    for here, copy in zip(has[2:], ycopy):
        @pl.when(here)
        def _():
            copy.start()
    for here, copy in zip((has[3], has[2]), ycopy):
        @pl.when(here)
        def _():
            copy.wait_recv()

    def y_halo(j, carry):
        left, right = carry
        i = 16 - j
        low = lane48 < 64
        u1[i, 1] = jnp.where(low, right, roll(left, -3, 1))
        w0[i, 1] = jnp.where(low, roll(right, -3, 1), roll(left, -6, 1))
        a_[i, 1] = jnp.where(low, roll(right, -6, 1), roll(left, -8, 1))
        return roll(left, -8, 1), roll(right, -8, 1)

    carry = (jnp.where(has[2], yr[1], 0.0), jnp.where(has[3], yr[0], 0.0))
    carry = lax.fori_loop(0, 3, y_halo, carry)

    ring = ((u1, 16, 2), (w0, 16, 2), (u1, 15, 1), (w0, 15, 1), (a_, 16, 1))
    top, low, columns = None, None, None
    at = 0
    for ref, i, depth in ring:
        t = roll(ref[i, 0, pl.ds(0, 8)], -at, 0)
        b = roll(ref[i, 0, pl.ds(40, 8)], at, 0)
        top = t if top is None else jnp.where(row8 < 8 - at, t, top)
        low = b if low is None else jnp.where(row8 >= at, b, low)
        at += depth
    for k in range(6):
        part, at = None, 0
        for ref, i, depth in ring:
            c = roll(ref[i, 1, pl.ds(8 * k, 8)], at + depth + 16 * k, 1)
            part = c if part is None else jnp.where(lane8 >= at + 16 * k, c, part)
            at += 2 * depth
        columns = part if columns is None else jnp.where(lane8 >= 16 * k, part, columns)
    gs[0], gs[1], gs[2] = top, low, columns
    gcopy.start()
    lax.fori_loop(3, 16, y_halo, carry)

    def sweep(old_u, new_u, old_w, new_w):
        def run(i, _):
            (c0, c1), (n0, n1) = stencil_full(old_u, i)
            new_u[i, 0] = KEEP * c0 + u1[i, 0] + a_[i, 0] * n0
            new_u[i, 1] = KEEP * c1 + u1[i, 1] + a_[i, 1] * n1
            (c0, c1), (n0, n1) = stencil_full(old_w, i)
            new_w[i, 0] = KEEP * c0 + a_[i, 0] * n0
            new_w[i, 1] = KEEP * c1 + a_[i, 1] * n1
            return 0
        return run

    def finish(i, _):
        z = source(i - 1)
        weight, s1 = a_[i, 0, OWN], u1[i, 0, OWN]
        c, n = stencil_own(u3, i)
        s4 = s1 + weight * n
        b, n = stencil_own(w2, i)
        w3 = KEEP * b + weight * n
        second = u2[i, 0, OWN]
        total = w0[i, 0, OWN] * s4 + w1[i, 0, OWN] * (c - KEEP * second) + b * (second - KEEP * s1) + w3 * s1
        rg[z] = (2.0 / RELAX) * jnp.exp(-2.0 * lr[z]) * total
        it[z] = jnp.where(ms[z] > 0, KEEP * c + s4, LAND * fo[z])
        return 0

    first = sweep(u1, u2, w0, w1)
    second = sweep(u2, u3, w1, w2)
    lax.fori_loop(1, 16, first, 0)
    lax.fori_loop(1, 15, second, 0)
    lax.fori_loop(1, 14, finish, 0)

    bulk, edge = pl.ds(3 * gz, 13), pl.ds(13 * (1 - gz), 3)
    stores = [pltpu.make_async_copy(v.at[part], h.at[part], out_sem.at[i])
              for i, (v, h, part) in enumerate(((it, it_h, bulk), (rg, rg_h, bulk), (it, it_h, edge), (rg, rg_h, edge)))]
    stores[0].start()
    stores[1].start()

    zcopy.wait_recv()
    for j in range(3):
        u1[17 + j, 0, OWN] = zr[j]
        w0[17 + j, 0, OWN] = zr[3 + j]
    for j in range(2):
        a_[17 + j, 0, OWN] = zr[6 + j]
    gcopy.wait_recv()
    top, low, columns = gr[0], gr[1], gr[2]
    at = 0
    for ref, i, depth in ring:
        ref[33 - i, 0, pl.ds(0, 8)] = roll(top, at, 0)
        ref[33 - i, 0, pl.ds(40, 8)] = roll(low, -at, 0)
        at += depth
    for k in range(6):
        at = 0
        for ref, i, depth in ring:
            ref[33 - i, 1, pl.ds(8 * k, 8)] = roll(columns, -(at + depth + 16 * k), 1)
            at += 2 * depth

    lax.fori_loop(16, 19, first, 0)
    lax.fori_loop(15, 18, second, 0)
    lax.fori_loop(14, 17, finish, 0)
    stores[2].start()
    stores[3].start()

    for here, copy in zip(has, xcopy + ycopy):
        @pl.when(here)
        def _():
            copy.wait_send()
    zcopy.wait_send()
    gcopy.wait_send()
    for store in stores:
        store.wait()


def solution(mesh):
    sizes = mesh.shape["gx"], mesh.shape["gy"]
    spec = P("gz", "gx", "gy")

    def body(log_range, sea_mask, forcing, cotangent):
        block = log_range.shape
        f32 = jnp.float32
        field = pltpu.VMEM((20, 2, 48, 128), f32)
        return pl.pallas_call(
            functools.partial(kernel, sizes),
            out_shape=[jax.ShapeDtypeStruct(block, f32)] * 2,
            in_specs=[pl.BlockSpec(memory_space=pl.ANY)] * 4,
            out_specs=[pl.BlockSpec(memory_space=pl.ANY)] * 2,
            scratch_shapes=[
                pltpu.VMEM(block, f32), pltpu.VMEM(block, jnp.int32), pltpu.VMEM(block, f32), pltpu.VMEM(block, f32),
                pltpu.VMEM(block, f32), pltpu.VMEM(block, f32),
                field, field, field, field, field, field, field,
                pltpu.VMEM((2, 16, 8, 128), f32), pltpu.VMEM((2, 16, 8, 128), f32),
                pltpu.VMEM((2, 48, 128), f32), pltpu.VMEM((2, 48, 128), f32),
                pltpu.VMEM((8, 32, 128), f32), pltpu.VMEM((8, 32, 128), f32),
                pltpu.VMEM((3, 8, 128), f32), pltpu.VMEM((3, 8, 128), f32),
                pltpu.SemaphoreType.DMA((4,)), pltpu.SemaphoreType.DMA((4,)), pltpu.SemaphoreType.DMA((2, 6)),
            ],
            compiler_params=pltpu.CompilerParams(collective_id=0, has_side_effects=True, vmem_limit_bytes=48 * 1024 * 1024),
            cost_estimate=pl.CostEstimate(flops=10_000_000, bytes_accessed=1_600_000, transcendentals=200_000),
        )(log_range, sea_mask, forcing, cotangent)

    return jax.shard_map(body, mesh=mesh, in_specs=(spec,) * 4, out_specs=(spec, spec), check_vma=False)
```

```python
import functools

import jax
import jax.numpy as jnp
from jax import lax
from jax.experimental import pallas as pl
from jax.experimental.pallas import tpu as pltpu
from jax.sharding import PartitionSpec as P

MESH = pl.DeviceIdType.MESH
RELAX = 0.9
KEEP = 1.0 - RELAX
TURNS = (4, 8, 8)
LAND = RELAX * (1.0 + KEEP + KEEP * KEEP + KEEP * KEEP * KEEP)
OWN = pl.ds(8, 32)


def roll(value, shift, axis):
    size = value.shape[axis]
    shift = shift % size
    return pltpu.roll(value, shift, axis) if shift else value


def stencil_full(ref, i):
    lane = lax.broadcasted_iota(jnp.int32, (48, 128), 1)
    first, last = lane == 0, lane == 127
    c0, c1 = ref[i, 0], ref[i, 1]
    r0, r1 = roll(c0, 1, 1), roll(c1, 1, 1)
    l0, l1 = roll(c0, -1, 1), roll(c1, -1, 1)
    n0 = ref[i - 1, 0] + ref[i + 1, 0] + (roll(c0, 1, 0) + roll(c0, -1, 0))
    n1 = ref[i - 1, 1] + ref[i + 1, 1] + (roll(c1, 1, 0) + roll(c1, -1, 0))
    n0 = n0 + jnp.where(first, r1, r0) + jnp.where(last, l1, l0)
    n1 = n1 + jnp.where(first, r0, r1) + jnp.where(last, l0, l1)
    return (c0, c1), (n0, n1)


def stencil_own(ref, i):
    lane = lax.broadcasted_iota(jnp.int32, (32, 128), 1)
    c = ref[i, 0]
    own = c[8:40]
    side = ref[i, 1, OWN]
    n = ref[i - 1, 0, OWN] + ref[i + 1, 0, OWN]
    n = n + (roll(c, 1, 0)[8:40] + roll(c, -1, 0)[8:40])
    n = n + jnp.where(lane == 0, roll(side, 1, 1), roll(own, 1, 1))
    n = n + jnp.where(lane == 127, roll(side, -1, 1), roll(own, -1, 1))
    return own, n


def kernel(sizes, lr_h, m_h, f_h, c_h, it, rg,
           lr, ms, fo, co, a_, u1, u2, u3, w0, w1, w2,
           xs, xr, ys, yr, zs, zr, gs, gr, in_sem, sem, ready):
    nx, ny = sizes
    gz, gx, gy = lax.axis_index("gz"), lax.axis_index("gx"), lax.axis_index("gy")
    has = [gx > 0, gx < nx - 1, gy > 0, gy < ny - 1]
    to = [{"gx": gx - 1}, {"gx": gx + 1}, {"gy": gy - 1}, {"gy": gy + 1}]
    partner = {"gz": 1 - gz}

    barrier = pltpu.get_barrier_semaphore()
    @pl.when(gz == 0)
    def _():
        pl.semaphore_signal(barrier, inc=1, device_id=partner, device_id_type=MESH)
    for here, device in zip(has, to):
        @pl.when(here)
        def _():
            pl.semaphore_signal(barrier, inc=1, device_id=device, device_id_type=MESH)

    loads = [pltpu.make_async_copy(h, v, in_sem.at[i]) for i, (h, v) in enumerate(((lr_h, lr), (m_h, ms), (f_h, fo), (c_h, co)))]
    for load in loads:
        load.start()

    def remote(src, dst, i, device):
        return pltpu.make_async_remote_copy(src_ref=src, dst_ref=dst, send_sem=sem.at[0, i], recv_sem=sem.at[1, i],
                                            device_id=device, device_id_type=MESH)

    xcopy = [remote(xs.at[0], xr.at[0], 0, to[0]), remote(xs.at[1], xr.at[1], 1, to[1])]
    ycopy = [remote(ys.at[0], yr.at[0], 2, to[2]), remote(ys.at[1], yr.at[1], 3, to[3])]
    zcopy = remote(zs, zr, 4, partner)
    gcopy = remote(gs, gr, 5, partner)

    def source(i):
        return jnp.where(gz == 0, i, 15 - i)

    row8 = lax.broadcasted_iota(jnp.int32, (8, 128), 0)
    lane8 = lax.broadcasted_iota(jnp.int32, (8, 128), 1)
    lane48 = lax.broadcasted_iota(jnp.int32, (48, 128), 1)
    zero = jnp.zeros((48, 128), jnp.float32)
    for ref in (u1, u2, u3, w0, w1, w2):
        ref[0, 0] = zero
        ref[0, 1] = zero
    for load in loads:
        load.wait()

    def prepare(i, _):
        z = source(i)
        mask = ms[z].astype(jnp.float32)
        inverse = 1.0 / (mask * (6.0 + jnp.exp(-2.0 * lr[z])) + (1.0 - mask))
        weight = RELAX * mask * inverse
        u, w = weight * fo[z], weight * co[z]
        a_[i + 1, 0, OWN] = weight
        u1[i + 1, 0, OWN] = u
        w0[i + 1, 0, OWN] = w
        up_u, up_w, up_a = u[:8], w[:8], weight[:8]
        dn_u, dn_w, dn_a = u[24:], w[24:], weight[24:]
        xs[0, i] = jnp.where(row8 < 3, up_u, jnp.where(row8 < 6, roll(up_w, 3, 0), roll(up_a, 6, 0)))
        xs[1, i] = jnp.where(row8 >= 5, dn_u, jnp.where(row8 >= 2, roll(dn_w, -3, 0), roll(dn_a, -6, 0)))
        return 0

    lax.fori_loop(0, 16, prepare, 0)
    for j in range(3):
        zs[j] = u1[16 - j, 0, OWN]
        zs[3 + j] = w0[16 - j, 0, OWN]
    for j in range(2):
        zs[6 + j] = a_[16 - j, 0, OWN]

    pl.semaphore_wait(barrier, gz + sum(h.astype(jnp.int32) for h in has))

    @pl.when(gz == 1)
    def _():
        pl.semaphore_signal(ready, inc=1, device_id=partner, device_id_type=MESH)

    turn = sum((gx * 8 // nx >= at).astype(jnp.int32) for at in TURNS)

    def send_layers(phase):
        @pl.when((gz == 1) & (turn == phase))
        def _():
            zcopy.start()

    for here, copy in zip(has[:2], xcopy):
        @pl.when(here)
        def _():
            copy.start()
    send_layers(0)

    for here, copy in zip((has[1], has[0]), xcopy):
        @pl.when(here)
        def _():
            copy.wait_recv()

    def x_halo(i, carry):
        right, left = carry
        low = jnp.where(has[1], xr[0, i], 0.0)
        top = jnp.where(has[0], xr[1, i], 0.0)
        u1[i + 1, 0, pl.ds(40, 8)] = low
        w0[i + 1, 0, pl.ds(40, 8)] = roll(low, -3, 0)
        a_[i + 1, 0, pl.ds(40, 8)] = roll(low, -6, 0)
        u1[i + 1, 0, pl.ds(0, 8)] = top
        w0[i + 1, 0, pl.ds(0, 8)] = roll(top, 3, 0)
        a_[i + 1, 0, pl.ds(0, 8)] = roll(top, 6, 0)
        u, w, weight = u1[i + 1, 0], w0[i + 1, 0], a_[i + 1, 0]
        to_right = jnp.where(lane48 < 3, roll(u, 3, 1), jnp.where(lane48 < 6, roll(w, 6, 1), roll(weight, 8, 1)))
        to_left = jnp.where(lane48 < 3, u, jnp.where(lane48 < 6, roll(w, 3, 1), roll(weight, 6, 1)))
        right = jnp.where(lane48 < 8, to_right, roll(right, 8, 1))
        left = jnp.where(lane48 < 8, to_left, roll(left, 8, 1))
        return right, left

    right, left = lax.fori_loop(0, 16, x_halo, (zero, zero))
    ys[1] = right
    ys[0] = left
    for here, copy in zip(has[2:], ycopy):
        @pl.when(here)
        def _():
            copy.start()
    send_layers(1)
    for here, copy in zip((has[3], has[2]), ycopy):
        @pl.when(here)
        def _():
            copy.wait_recv()

    def y_halo(j, carry):
        left, right = carry
        i = 16 - j
        low = lane48 < 64
        u1[i, 1] = jnp.where(low, right, roll(left, -3, 1))
        w0[i, 1] = jnp.where(low, roll(right, -3, 1), roll(left, -6, 1))
        a_[i, 1] = jnp.where(low, roll(right, -6, 1), roll(left, -8, 1))
        return roll(left, -8, 1), roll(right, -8, 1)

    carry = (jnp.where(has[2], yr[1], 0.0), jnp.where(has[3], yr[0], 0.0))
    carry = lax.fori_loop(0, 3, y_halo, carry)

    ring = ((u1, 16, 2), (w0, 16, 2), (u1, 15, 1), (w0, 15, 1), (a_, 16, 1))
    top, low, columns = None, None, None
    at = 0
    for ref, i, depth in ring:
        t = roll(ref[i, 0, pl.ds(0, 8)], -at, 0)
        b = roll(ref[i, 0, pl.ds(40, 8)], at, 0)
        top = t if top is None else jnp.where(row8 < 8 - at, t, top)
        low = b if low is None else jnp.where(row8 >= at, b, low)
        at += depth
    for k in range(6):
        part, at = None, 0
        for ref, i, depth in ring:
            c = roll(ref[i, 1, pl.ds(8 * k, 8)], at + depth + 16 * k, 1)
            part = c if part is None else jnp.where(lane8 >= at + 16 * k, c, part)
            at += 2 * depth
        columns = part if columns is None else jnp.where(lane8 >= 16 * k, part, columns)
    gs[0], gs[1], gs[2] = top, low, columns
    send_layers(2)

    @pl.when(gz == 0)
    def _():
        pl.semaphore_wait(ready, 1)
        zcopy.start()

    gcopy.start()
    lax.fori_loop(3, 16, y_halo, carry)

    def sweep(old_u, new_u, old_w, new_w):
        def run(i, _):
            (c0, c1), (n0, n1) = stencil_full(old_u, i)
            new_u[i, 0] = KEEP * c0 + u1[i, 0] + a_[i, 0] * n0
            new_u[i, 1] = KEEP * c1 + u1[i, 1] + a_[i, 1] * n1
            (c0, c1), (n0, n1) = stencil_full(old_w, i)
            new_w[i, 0] = KEEP * c0 + a_[i, 0] * n0
            new_w[i, 1] = KEEP * c1 + a_[i, 1] * n1
            return 0
        return run

    def finish(i, _):
        z = source(i - 1)
        weight, s1 = a_[i, 0, OWN], u1[i, 0, OWN]
        c, n = stencil_own(u3, i)
        s4 = s1 + weight * n
        b, n = stencil_own(w2, i)
        w3 = KEEP * b + weight * n
        second = u2[i, 0, OWN]
        total = w0[i, 0, OWN] * s4 + w1[i, 0, OWN] * (c - KEEP * second) + b * (second - KEEP * s1) + w3 * s1
        rg[z] = (2.0 / RELAX) * jnp.exp(-2.0 * lr[z]) * total
        it[z] = jnp.where(ms[z] > 0, KEEP * c + s4, LAND * fo[z])
        return 0

    first = sweep(u1, u2, w0, w1)
    second = sweep(u2, u3, w1, w2)
    lax.fori_loop(1, 16, first, 0)
    send_layers(3)
    lax.fori_loop(1, 15, second, 0)
    lax.fori_loop(1, 14, finish, 0)

    zcopy.wait_recv()
    for j in range(3):
        u1[17 + j, 0, OWN] = zr[j]
        w0[17 + j, 0, OWN] = zr[3 + j]
    for j in range(2):
        a_[17 + j, 0, OWN] = zr[6 + j]
    gcopy.wait_recv()
    top, low, columns = gr[0], gr[1], gr[2]
    at = 0
    for ref, i, depth in ring:
        ref[33 - i, 0, pl.ds(0, 8)] = roll(top, at, 0)
        ref[33 - i, 0, pl.ds(40, 8)] = roll(low, -at, 0)
        at += depth
    for k in range(6):
        at = 0
        for ref, i, depth in ring:
            ref[33 - i, 1, pl.ds(8 * k, 8)] = roll(columns, -(at + depth + 16 * k), 1)
            at += 2 * depth

    lax.fori_loop(16, 19, first, 0)
    lax.fori_loop(15, 18, second, 0)
    lax.fori_loop(14, 17, finish, 0)

    for here, copy in zip(has, xcopy + ycopy):
        @pl.when(here)
        def _():
            copy.wait_send()
    zcopy.wait_send()
    gcopy.wait_send()


def solution(mesh):
    sizes = mesh.shape["gx"], mesh.shape["gy"]
    spec = P("gz", "gx", "gy")

    def body(log_range, sea_mask, forcing, cotangent):
        block = log_range.shape
        f32 = jnp.float32
        field = pltpu.VMEM((20, 2, 48, 128), f32)
        return pl.pallas_call(
            functools.partial(kernel, sizes),
            out_shape=[pltpu.VMEM(block, f32)] * 2,
            in_specs=[pl.BlockSpec(memory_space=pltpu.HBM)] * 4,
            out_specs=[pl.BlockSpec(memory_space=pltpu.VMEM)] * 2,
            scratch_shapes=[
                pltpu.VMEM(block, f32), pltpu.VMEM(block, jnp.int32), pltpu.VMEM(block, f32), pltpu.VMEM(block, f32),
                field, field, field, field, field, field, field,
                pltpu.VMEM((2, 16, 8, 128), f32), pltpu.VMEM((2, 16, 8, 128), f32),
                pltpu.VMEM((2, 48, 128), f32), pltpu.VMEM((2, 48, 128), f32),
                pltpu.VMEM((8, 32, 128), f32), pltpu.VMEM((8, 32, 128), f32),
                pltpu.VMEM((3, 8, 128), f32), pltpu.VMEM((3, 8, 128), f32),
                pltpu.SemaphoreType.DMA((4,)), pltpu.SemaphoreType.DMA((2, 6)),
                pltpu.SemaphoreType.REGULAR,
            ],
            compiler_params=pltpu.CompilerParams(collective_id=0, has_side_effects=True, vmem_limit_bytes=48 * 1024 * 1024),
            cost_estimate=pl.CostEstimate(flops=10_000_000, bytes_accessed=1_600_000, transcendentals=200_000),
        )(*(pltpu.with_memory_space_constraint(x, pltpu.HBM) for x in (log_range, sea_mask, forcing, cotangent)))

    return jax.shard_map(body, mesh=mesh, in_specs=(spec,) * 4, out_specs=(spec, spec), check_vma=False)
```

```python
import functools

import jax
import jax.numpy as jnp
from jax import lax
from jax.experimental import pallas as pl
from jax.experimental.pallas import tpu as pltpu
from jax.sharding import PartitionSpec as P

MESH = pl.DeviceIdType.MESH
SIDES = ((-1, 0), (1, 0), (0, -1), (0, 1), (-1, -1), (1, -1), (-1, 1), (1, 1))
RELAX = 0.9
KEEP = 1.0 - RELAX
TURNS = (0, 0, 0, 0, 0, 1, 2, 2)
LAND = RELAX * (1.0 + KEEP + KEEP * KEEP + KEEP * KEEP * KEEP)
OWN = pl.ds(8, 32)


def roll(value, shift, axis):
    size = value.shape[axis]
    shift = shift % size
    return pltpu.roll(value, shift, axis) if shift else value


def stencil_full(ref, i):
    lane = lax.broadcasted_iota(jnp.int32, (48, 128), 1)
    first, last = lane == 0, lane == 127
    c0, c1 = ref[i, 0], ref[i, 1]
    r0, r1 = roll(c0, 1, 1), roll(c1, 1, 1)
    l0, l1 = roll(c0, -1, 1), roll(c1, -1, 1)
    n0 = ref[i - 1, 0] + ref[i + 1, 0] + (roll(c0, 1, 0) + roll(c0, -1, 0))
    n1 = ref[i - 1, 1] + ref[i + 1, 1] + (roll(c1, 1, 0) + roll(c1, -1, 0))
    n0 = n0 + jnp.where(first, r1, r0) + jnp.where(last, l1, l0)
    n1 = n1 + jnp.where(first, r0, r1) + jnp.where(last, l0, l1)
    return (c0, c1), (n0, n1)


def stencil_own(ref, i):
    lane = lax.broadcasted_iota(jnp.int32, (32, 128), 1)
    c = ref[i, 0]
    own = c[8:40]
    side = ref[i, 1, OWN]
    n = ref[i - 1, 0, OWN] + ref[i + 1, 0, OWN]
    n = n + (roll(c, 1, 0)[8:40] + roll(c, -1, 0)[8:40])
    n = n + jnp.where(lane == 0, roll(side, 1, 1), roll(own, 1, 1))
    n = n + jnp.where(lane == 127, roll(side, -1, 1), roll(own, -1, 1))
    return own, n


def kernel(sizes, lr_h, m_h, f_h, c_h, it, rg,
           lr, ms, fo, co, a_, u1, u2, u3, w0, w1, w2,
           xs, xr, ys, yr, zs, zr, gs, gr, in_sem, sem, ready):
    nx, ny = sizes
    gz, gx, gy = lax.axis_index("gz"), lax.axis_index("gx"), lax.axis_index("gy")
    partner = {"gz": 1 - gz}
    has = {}
    for x, y in SIDES:
        here = []
        if x:
            here.append(gx > 0 if x < 0 else gx < nx - 1)
        if y:
            here.append(gy > 0 if y < 0 else gy < ny - 1)
        has[x, y] = here[0] if len(here) == 1 else here[0] & here[1]

    def at(side):
        return {"gx": gx + side[0], "gy": gy + side[1]}

    barrier = pltpu.get_barrier_semaphore()

    @pl.when(gz == 0)
    def _():
        pl.semaphore_signal(barrier, inc=1, device_id=partner, device_id_type=MESH)

    for side in SIDES:
        @pl.when(has[side])
        def _():
            pl.semaphore_signal(barrier, inc=1, device_id=at(side), device_id_type=MESH)

    loads = [pltpu.make_async_copy(h, v, in_sem.at[i]) for i, (h, v) in enumerate(((lr_h, lr), (m_h, ms), (f_h, fo), (c_h, co)))]
    for load in loads:
        load.start()

    def remote(src, dst, i, device):
        return pltpu.make_async_remote_copy(src_ref=src, dst_ref=dst, send_sem=sem.at[0, i], recv_sem=sem.at[1, i],
                                            device_id=device, device_id_type=MESH)

    low, mid, top = pl.ds(40, 8), pl.ds(8, 32), pl.ds(0, 8)
    first8, last8 = pl.ds(0, 8), pl.ds(24, 8)
    copies = {}
    for i, (side, src, dst) in enumerate((
        ((-1, 0), xs.at[0], xr.at[0]), ((1, 0), xs.at[1], xr.at[1]),
        ((0, -1), ys.at[0], yr.at[0, mid]), ((0, 1), ys.at[1], yr.at[1, mid]),
        ((-1, -1), ys.at[0, first8], yr.at[0, low]), ((1, -1), ys.at[0, last8], yr.at[0, top]),
        ((-1, 1), ys.at[1, first8], yr.at[1, low]), ((1, 1), ys.at[1, last8], yr.at[1, top]),
    )):
        copies[side] = remote(src, dst, i, at(side))
    zcopy = remote(zs, zr, 8, partner)
    gcopy = remote(gs, gr, 9, partner)

    def source(i):
        return jnp.where(gz == 0, i, 15 - i)

    row8 = lax.broadcasted_iota(jnp.int32, (8, 128), 0)
    lane8 = lax.broadcasted_iota(jnp.int32, (8, 128), 1)
    lane32 = lax.broadcasted_iota(jnp.int32, (32, 128), 1)
    lane48 = lax.broadcasted_iota(jnp.int32, (48, 128), 1)
    zero = jnp.zeros((48, 128), jnp.float32)
    for ref in (u1, u2, u3, w0, w1, w2):
        ref[0, 0] = zero
        ref[0, 1] = zero
    for load in loads:
        load.wait()

    def prepare(i, carry):
        left, right = carry
        z = source(i)
        mask = ms[z].astype(jnp.float32)
        inverse = 1.0 / (mask * (6.0 + jnp.exp(-2.0 * lr[z])) + (1.0 - mask))
        weight = RELAX * mask * inverse
        u, w = weight * fo[z], weight * co[z]
        a_[i + 1, 0, OWN] = weight
        u1[i + 1, 0, OWN] = u
        w0[i + 1, 0, OWN] = w
        up_u, up_w, up_a = u[:8], w[:8], weight[:8]
        dn_u, dn_w, dn_a = u[24:], w[24:], weight[24:]
        xs[0, i] = jnp.where(row8 < 3, up_u, jnp.where(row8 < 6, roll(up_w, 3, 0), roll(up_a, 6, 0)))
        xs[1, i] = jnp.where(row8 >= 5, dn_u, jnp.where(row8 >= 2, roll(dn_w, -3, 0), roll(dn_a, -6, 0)))
        to_right = jnp.where(lane32 < 3, roll(u, 3, 1), jnp.where(lane32 < 6, roll(w, 6, 1), roll(weight, 8, 1)))
        to_left = jnp.where(lane32 < 3, u, jnp.where(lane32 < 6, roll(w, 3, 1), roll(weight, 6, 1)))
        left = jnp.where(lane32 < 8, to_left, roll(left, 8, 1))
        right = jnp.where(lane32 < 8, to_right, roll(right, 8, 1))
        return left, right

    left, right = lax.fori_loop(0, 16, prepare, (zero[:32], zero[:32]))
    ys[0] = left
    ys[1] = right
    for j, (ref, i) in enumerate(((u1, 16), (u1, 15), (w0, 16), (w0, 15), (a_, 16))):
        zs[j] = ref[i, 0, OWN]

    pl.semaphore_wait(barrier, gz + sum(h.astype(jnp.int32) for h in has.values()))

    @pl.when(gz == 1)
    def _():
        pl.semaphore_signal(ready, inc=1, device_id=partner, device_id_type=MESH)

    place = gx * 8 // nx
    turn = sum(jnp.where(place == i, t, 0) for i, t in enumerate(TURNS) if t)

    def send_layers(phase):
        @pl.when((gz == 1) & (turn == phase))
        def _():
            zcopy.start()
            if phase > 1:
                gcopy.start()

    for side in SIDES:
        @pl.when(has[side])
        def _():
            copies[side].start()
    send_layers(0)

    for side in SIDES:
        @pl.when(has[-side[0], -side[1]])
        def _():
            copies[side].wait_recv()
    send_layers(1)

    def halo(j, carry):
        left, right = carry
        i = 16 - j
        below = jnp.where(has[1, 0], xr[0, i - 1], 0.0)
        above = jnp.where(has[-1, 0], xr[1, i - 1], 0.0)
        u1[i, 0, low] = below
        w0[i, 0, low] = roll(below, -3, 0)
        a_[i, 0, low] = roll(below, -6, 0)
        u1[i, 0, top] = above
        w0[i, 0, top] = roll(above, 3, 0)
        a_[i, 0, top] = roll(above, 6, 0)
        half = lane48 < 64
        u1[i, 1] = jnp.where(half, right, roll(left, -3, 1))
        w0[i, 1] = jnp.where(half, roll(right, -3, 1), roll(left, -6, 1))
        a_[i, 1] = jnp.where(half, roll(right, -6, 1), roll(left, -8, 1))
        return roll(left, -8, 1), roll(right, -8, 1)

    def arrived(slot, y):
        parts = [jnp.where(has[x, y], yr[slot, rows], 0.0) for x, rows in ((-1, top), (0, mid), (1, low))]
        return jnp.concatenate(parts, axis=0)

    carry = lax.fori_loop(0, 3, halo, (arrived(1, -1), arrived(0, 1)))

    def sweep(old_u, new_u, old_w, new_w):
        def run(i, _):
            (c0, c1), (n0, n1) = stencil_full(old_u, i)
            new_u[i, 0] = KEEP * c0 + u1[i, 0] + a_[i, 0] * n0
            new_u[i, 1] = KEEP * c1 + u1[i, 1] + a_[i, 1] * n1
            (c0, c1), (n0, n1) = stencil_full(old_w, i)
            new_w[i, 0] = KEEP * c0 + a_[i, 0] * n0
            new_w[i, 1] = KEEP * c1 + a_[i, 1] * n1
            return 0
        return run

    def finish(i, _):
        z = source(i - 1)
        weight, s1 = a_[i, 0, OWN], u1[i, 0, OWN]
        c, n = stencil_own(u3, i)
        s4 = s1 + weight * n
        b, n = stencil_own(w2, i)
        w3 = KEEP * b + weight * n
        second = u2[i, 0, OWN]
        total = w0[i, 0, OWN] * s4 + w1[i, 0, OWN] * (c - KEEP * second) + b * (second - KEEP * s1) + w3 * s1
        rg[z] = (2.0 / RELAX) * jnp.exp(-2.0 * lr[z]) * total
        it[z] = jnp.where(ms[z] > 0, KEEP * c + s4, LAND * fo[z])
        return 0

    first = sweep(u1, u2, w0, w1)
    second = sweep(u2, u3, w1, w2)
    first(15, 0)
    ring = ((u1, 16, 2), (w0, 16, 2), (u1, 15, 1), (w0, 15, 1), (a_, 16, 1))
    above, below, columns = None, None, None
    at = 0
    for ref, i, depth in ring:
        t = roll(ref[i, 0, top], -at, 0)
        b = roll(ref[i, 0, low], at, 0)
        above = t if above is None else jnp.where(row8 < 8 - at, t, above)
        below = b if below is None else jnp.where(row8 >= at, b, below)
        at += depth
    for k in range(6):
        part, at = None, 0
        for ref, i, depth in ring:
            c = roll(ref[i, 1, pl.ds(8 * k, 8)], at + depth + 16 * k, 1)
            part = c if part is None else jnp.where(lane8 >= at + 16 * k, c, part)
            at += 2 * depth
        columns = part if columns is None else jnp.where(lane8 >= 16 * k, part, columns)
    gs[first8] = above
    gs[pl.ds(8, 8)] = below
    gs[pl.ds(16, 8)] = columns
    gs[pl.ds(24, 32)] = u2[15, 0, OWN]
    gs[pl.ds(56, 32)] = w1[15, 0, OWN]
    @pl.when((gz == 1) & (turn < 2))
    def _():
        gcopy.start()

    send_layers(2)

    lax.fori_loop(3, 16, halo, carry)
    send_layers(3)
    lax.fori_loop(1, 6, first, 0)
    send_layers(4)
    lax.fori_loop(6, 15, first, 0)

    @pl.when(gz == 0)
    def _():
        pl.semaphore_wait(ready, 1)
        zcopy.start()
        gcopy.start()

    lax.fori_loop(1, 15, second, 0)
    lax.fori_loop(1, 14, finish, 0)

    zcopy.wait_recv()
    for j, (ref, i) in enumerate(((u1, 17), (u1, 18), (w0, 17), (w0, 18), (a_, 17))):
        ref[i, 0, OWN] = zr[j]
    gcopy.wait_recv()
    above, below, columns = gr[first8], gr[pl.ds(8, 8)], gr[pl.ds(16, 8)]
    u2[18, 0, OWN] = gr[pl.ds(24, 32)]
    w1[18, 0, OWN] = gr[pl.ds(56, 32)]
    at = 0
    for ref, i, depth in ring:
        ref[33 - i, 0, top] = roll(above, at, 0)
        ref[33 - i, 0, low] = roll(below, -at, 0)
        at += depth
    for k in range(6):
        at = 0
        for ref, i, depth in ring:
            ref[33 - i, 1, pl.ds(8 * k, 8)] = roll(columns, -(at + depth + 16 * k), 1)
            at += 2 * depth

    lax.fori_loop(16, 18, first, 0)
    lax.fori_loop(15, 18, second, 0)
    lax.fori_loop(14, 17, finish, 0)

    for side in SIDES:
        @pl.when(has[side])
        def _():
            copies[side].wait_send()
    zcopy.wait_send()
    gcopy.wait_send()


def solution(mesh):
    sizes = mesh.shape["gx"], mesh.shape["gy"]
    spec = P("gz", "gx", "gy")

    def body(log_range, sea_mask, forcing, cotangent):
        block = log_range.shape
        f32 = jnp.float32
        field = pltpu.VMEM((19, 2, 48, 128), f32)
        return pl.pallas_call(
            functools.partial(kernel, sizes),
            out_shape=[pltpu.VMEM(block, f32)] * 2,
            in_specs=[pl.BlockSpec(memory_space=pltpu.HBM)] * 4,
            out_specs=[pl.BlockSpec(memory_space=pltpu.VMEM)] * 2,
            scratch_shapes=[
                pltpu.VMEM(block, f32), pltpu.VMEM(block, jnp.int32), pltpu.VMEM(block, f32), pltpu.VMEM(block, f32),
                field, field, field, field, field, field, field,
                pltpu.VMEM((2, 16, 8, 128), f32), pltpu.VMEM((2, 16, 8, 128), f32),
                pltpu.VMEM((2, 32, 128), f32), pltpu.VMEM((2, 48, 128), f32),
                pltpu.VMEM((5, 32, 128), f32), pltpu.VMEM((5, 32, 128), f32),
                pltpu.VMEM((88, 128), f32), pltpu.VMEM((88, 128), f32),
                pltpu.SemaphoreType.DMA((4,)), pltpu.SemaphoreType.DMA((2, 10)),
                pltpu.SemaphoreType.REGULAR,
            ],
            compiler_params=pltpu.CompilerParams(collective_id=0, has_side_effects=True, vmem_limit_bytes=48 * 1024 * 1024),
            cost_estimate=pl.CostEstimate(flops=10_000_000, bytes_accessed=1_600_000, transcendentals=200_000),
        )(*(pltpu.with_memory_space_constraint(x, pltpu.HBM) for x in (log_range, sea_mask, forcing, cotangent)))

    def store(it, rg, it_h, rg_h, sem):
        copies = [pltpu.make_async_copy(v.at[pl.ds(16 * h, 16)], o.at[pl.ds(16 * h, 16)], sem.at[i, h])
                  for i, (v, o) in enumerate(((it, it_h), (rg, rg_h))) for h in range(1)]
        for copy in copies:
            copy.start()
        for copy in copies:
            copy.wait()

    def whole(*args):
        parts = body(*args)
        parts = [pltpu.with_memory_space_constraint(x, pltpu.VMEM) for x in parts]
        return pl.pallas_call(store, out_shape=[jax.ShapeDtypeStruct(x.shape, jnp.float32) for x in parts],
                              in_specs=[pl.BlockSpec(memory_space=pltpu.VMEM)] * 2,
                              out_specs=[pl.BlockSpec(memory_space=pl.ANY)] * 2,
                              scratch_shapes=[pltpu.SemaphoreType.DMA((2, 1))])(*parts)

    return jax.shard_map(whole, mesh=mesh, in_specs=(spec,) * 4, out_specs=(spec, spec), check_vma=False)
```

```python
import functools

import jax
import jax.numpy as jnp
from jax import lax
from jax.experimental import pallas as pl
from jax.experimental.pallas import tpu as pltpu
from jax.sharding import PartitionSpec as P

MESH = pl.DeviceIdType.MESH
SIDES = ((-1, 0), (1, 0), (0, -1), (0, 1), (-1, -1), (1, -1), (-1, 1), (1, 1))
RELAX = 0.9
KEEP = 1.0 - RELAX
TURNS = (0, 0, 0, 0, 0, 2, 2, 2)
LAND = RELAX * (1.0 + KEEP + KEEP * KEEP + KEEP * KEEP * KEEP)
OWN = pl.ds(8, 32)


def roll(value, shift, axis):
    size = value.shape[axis]
    shift = shift % size
    return pltpu.roll(value, shift, axis) if shift else value


def stencil_full(ref, i):
    lane = lax.broadcasted_iota(jnp.int32, (48, 128), 1)
    first, last = lane == 0, lane == 127
    c0, c1 = ref[i, 0], ref[i, 1]
    r0, r1 = roll(c0, 1, 1), roll(c1, 1, 1)
    l0, l1 = roll(c0, -1, 1), roll(c1, -1, 1)
    n0 = ref[i - 1, 0] + ref[i + 1, 0] + (roll(c0, 1, 0) + roll(c0, -1, 0))
    n1 = ref[i - 1, 1] + ref[i + 1, 1] + (roll(c1, 1, 0) + roll(c1, -1, 0))
    n0 = n0 + jnp.where(first, r1, r0) + jnp.where(last, l1, l0)
    n1 = n1 + jnp.where(first, r0, r1) + jnp.where(last, l0, l1)
    return (c0, c1), (n0, n1)


def stencil_own(ref, i):
    lane = lax.broadcasted_iota(jnp.int32, (32, 128), 1)
    c = ref[i, 0]
    own = c[8:40]
    side = ref[i, 1, OWN]
    n = ref[i - 1, 0, OWN] + ref[i + 1, 0, OWN]
    n = n + (roll(c, 1, 0)[8:40] + roll(c, -1, 0)[8:40])
    n = n + jnp.where(lane == 0, roll(side, 1, 1), roll(own, 1, 1))
    n = n + jnp.where(lane == 127, roll(side, -1, 1), roll(own, -1, 1))
    return own, n


def kernel(sizes, lr_h, m_h, f_h, c_h, it, rg,
           lr, ms, fo, co, a_, u1, u2, u3, w0, w1, w2,
           xs, xr, ys, yr, zs, zr, gs, gr, in_sem, sem, ready):
    nx, ny = sizes
    gz, gx, gy = lax.axis_index("gz"), lax.axis_index("gx"), lax.axis_index("gy")
    partner = {"gz": 1 - gz}
    has = {}
    for x, y in SIDES:
        here = []
        if x:
            here.append(gx > 0 if x < 0 else gx < nx - 1)
        if y:
            here.append(gy > 0 if y < 0 else gy < ny - 1)
        has[x, y] = here[0] if len(here) == 1 else here[0] & here[1]

    def at(side):
        return {"gx": gx + side[0], "gy": gy + side[1]}

    barrier = pltpu.get_barrier_semaphore()

    @pl.when(gz == 0)
    def _():
        pl.semaphore_signal(barrier, inc=1, device_id=partner, device_id_type=MESH)

    for side in SIDES:
        @pl.when(has[side])
        def _():
            pl.semaphore_signal(barrier, inc=1, device_id=at(side), device_id_type=MESH)

    loads = [pltpu.make_async_copy(h, v, in_sem.at[i]) for i, (h, v) in enumerate(((lr_h, lr), (m_h, ms), (f_h, fo), (c_h, co)))]
    for load in loads:
        load.start()

    def remote(src, dst, i, device):
        return pltpu.make_async_remote_copy(src_ref=src, dst_ref=dst, send_sem=sem.at[0, i], recv_sem=sem.at[1, i],
                                            device_id=device, device_id_type=MESH)

    low, mid, top = pl.ds(40, 8), pl.ds(8, 32), pl.ds(0, 8)
    first8, last8 = pl.ds(0, 8), pl.ds(24, 8)
    near, rest = pl.ds(13, 3), pl.ds(0, 13)
    copies = {}
    for i, (side, src, dst) in enumerate((
        ((-1, 0), xs.at[0, near], xr.at[0, near]), ((1, 0), xs.at[1, near], xr.at[1, near]),
        ((0, -1), ys.at[0], yr.at[0, mid]), ((0, 1), ys.at[1], yr.at[1, mid]),
        ((-1, -1), ys.at[0, first8], yr.at[0, low]), ((1, -1), ys.at[0, last8], yr.at[0, top]),
        ((-1, 1), ys.at[1, first8], yr.at[1, low]), ((1, 1), ys.at[1, last8], yr.at[1, top]),
    )):
        copies[side] = remote(src, dst, i, at(side))
    far = {side: remote(xs.at[i, rest], xr.at[i, rest], 10 + i, at(side)) for i, side in enumerate(SIDES[:2])}
    zcopy = remote(zs, zr, 8, partner)
    gcopy = remote(gs, gr, 9, partner)

    def source(i):
        return jnp.where(gz == 0, i, 15 - i)

    row8 = lax.broadcasted_iota(jnp.int32, (8, 128), 0)
    lane8 = lax.broadcasted_iota(jnp.int32, (8, 128), 1)
    lane32 = lax.broadcasted_iota(jnp.int32, (32, 128), 1)
    lane48 = lax.broadcasted_iota(jnp.int32, (48, 128), 1)
    zero = jnp.zeros((48, 128), jnp.float32)
    for ref in (u1, u2, u3, w0, w1, w2):
        ref[0, 0] = zero
        ref[0, 1] = zero
    for load in loads:
        load.wait()

    def prepare(i, carry):
        left, right = carry
        z = source(i)
        mask = ms[z].astype(jnp.float32)
        inverse = 1.0 / (mask * (6.0 + jnp.exp(-2.0 * lr[z])) + (1.0 - mask))
        weight = RELAX * mask * inverse
        u, w = weight * fo[z], weight * co[z]
        a_[i + 1, 0, OWN] = weight
        u1[i + 1, 0, OWN] = u
        w0[i + 1, 0, OWN] = w
        up_u, up_w, up_a = u[:8], w[:8], weight[:8]
        dn_u, dn_w, dn_a = u[24:], w[24:], weight[24:]
        xs[0, i] = jnp.where(row8 < 3, up_u, jnp.where(row8 < 6, roll(up_w, 3, 0), roll(up_a, 6, 0)))
        xs[1, i] = jnp.where(row8 >= 5, dn_u, jnp.where(row8 >= 2, roll(dn_w, -3, 0), roll(dn_a, -6, 0)))
        to_right = jnp.where(lane32 < 3, roll(u, 3, 1), jnp.where(lane32 < 6, roll(w, 6, 1), roll(weight, 8, 1)))
        to_left = jnp.where(lane32 < 3, u, jnp.where(lane32 < 6, roll(w, 3, 1), roll(weight, 6, 1)))
        left = jnp.where(lane32 < 8, to_left, roll(left, 8, 1))
        right = jnp.where(lane32 < 8, to_right, roll(right, 8, 1))
        return left, right

    left, right = lax.fori_loop(0, 16, prepare, (zero[:32], zero[:32]))
    ys[0] = left
    ys[1] = right
    for j, (ref, i) in enumerate(((u1, 16), (u1, 15), (w0, 16), (w0, 15), (a_, 16))):
        zs[j] = ref[i, 0, OWN]

    pl.semaphore_wait(barrier, gz + sum(h.astype(jnp.int32) for h in has.values()))

    @pl.when(gz == 1)
    def _():
        pl.semaphore_signal(ready, inc=1, device_id=partner, device_id_type=MESH)

    place = gx * 8 // nx
    turn = sum(jnp.where(place == i, t, 0) for i, t in enumerate(TURNS) if t)

    def send_layers(phase):
        @pl.when((gz == 1) & (turn == phase))
        def _():
            zcopy.start()
            if phase > 1:
                gcopy.start()

    for side in SIDES:
        @pl.when(has[side])
        def _():
            copies[side].start()
    send_layers(0)
    for side in far:
        @pl.when(has[side])
        def _():
            far[side].start()

    for side in SIDES:
        @pl.when(has[-side[0], -side[1]])
        def _():
            copies[side].wait_recv()
    send_layers(1)

    def halo(j, carry):
        left, right = carry
        i = 16 - j
        below = jnp.where(has[1, 0], xr[0, i - 1], 0.0)
        above = jnp.where(has[-1, 0], xr[1, i - 1], 0.0)
        u1[i, 0, low] = below
        w0[i, 0, low] = roll(below, -3, 0)
        a_[i, 0, low] = roll(below, -6, 0)
        u1[i, 0, top] = above
        w0[i, 0, top] = roll(above, 3, 0)
        a_[i, 0, top] = roll(above, 6, 0)
        half = lane48 < 64
        u1[i, 1] = jnp.where(half, right, roll(left, -3, 1))
        w0[i, 1] = jnp.where(half, roll(right, -3, 1), roll(left, -6, 1))
        a_[i, 1] = jnp.where(half, roll(right, -6, 1), roll(left, -8, 1))
        return roll(left, -8, 1), roll(right, -8, 1)

    def arrived(slot, y):
        parts = [jnp.where(has[x, y], yr[slot, rows], 0.0) for x, rows in ((-1, top), (0, mid), (1, low))]
        return jnp.concatenate(parts, axis=0)

    carry = lax.fori_loop(0, 3, halo, (arrived(1, -1), arrived(0, 1)))

    def sweep(old_u, new_u, old_w, new_w):
        def run(i, _):
            (c0, c1), (n0, n1) = stencil_full(old_u, i)
            new_u[i, 0] = KEEP * c0 + u1[i, 0] + a_[i, 0] * n0
            new_u[i, 1] = KEEP * c1 + u1[i, 1] + a_[i, 1] * n1
            (c0, c1), (n0, n1) = stencil_full(old_w, i)
            new_w[i, 0] = KEEP * c0 + a_[i, 0] * n0
            new_w[i, 1] = KEEP * c1 + a_[i, 1] * n1
            return 0
        return run

    def finish(i, _):
        z = source(i - 1)
        weight, s1 = a_[i, 0, OWN], u1[i, 0, OWN]
        c, n = stencil_own(u3, i)
        s4 = s1 + weight * n
        b, n = stencil_own(w2, i)
        w3 = KEEP * b + weight * n
        second = u2[i, 0, OWN]
        total = w0[i, 0, OWN] * s4 + w1[i, 0, OWN] * (c - KEEP * second) + b * (second - KEEP * s1) + w3 * s1
        rg[z] = (2.0 / RELAX) * jnp.exp(-2.0 * lr[z]) * total
        it[z] = jnp.where(ms[z] > 0, KEEP * c + s4, LAND * fo[z])
        return 0

    first = sweep(u1, u2, w0, w1)
    second = sweep(u2, u3, w1, w2)
    first(15, 0)
    ring = ((u1, 16, 2), (w0, 16, 2), (u1, 15, 1), (w0, 15, 1), (a_, 16, 1))
    above, below, columns = None, None, None
    at = 0
    for ref, i, depth in ring:
        t = roll(ref[i, 0, top], -at, 0)
        b = roll(ref[i, 0, low], at, 0)
        above = t if above is None else jnp.where(row8 < 8 - at, t, above)
        below = b if below is None else jnp.where(row8 >= at, b, below)
        at += depth
    for k in range(6):
        part, at = None, 0
        for ref, i, depth in ring:
            c = roll(ref[i, 1, pl.ds(8 * k, 8)], at + depth + 16 * k, 1)
            part = c if part is None else jnp.where(lane8 >= at + 16 * k, c, part)
            at += 2 * depth
        columns = part if columns is None else jnp.where(lane8 >= 16 * k, part, columns)
    gs[first8] = above
    gs[pl.ds(8, 8)] = below
    gs[pl.ds(16, 8)] = columns
    gs[pl.ds(24, 32)] = u2[15, 0, OWN]
    gs[pl.ds(56, 32)] = w1[15, 0, OWN]
    @pl.when((gz == 1) & (turn < 2))
    def _():
        gcopy.start()

    send_layers(2)

    for side in far:
        @pl.when(has[-side[0], -side[1]])
        def _():
            far[side].wait_recv()
    lax.fori_loop(3, 16, halo, carry)
    send_layers(3)
    lax.fori_loop(1, 6, first, 0)
    send_layers(4)
    lax.fori_loop(6, 15, first, 0)

    @pl.when(gz == 0)
    def _():
        pl.semaphore_wait(ready, 1)
        zcopy.start()
        gcopy.start()

    lax.fori_loop(1, 15, second, 0)
    lax.fori_loop(1, 14, finish, 0)

    zcopy.wait_recv()
    for j, (ref, i) in enumerate(((u1, 17), (u1, 18), (w0, 17), (w0, 18), (a_, 17))):
        ref[i, 0, OWN] = zr[j]
    gcopy.wait_recv()
    above, below, columns = gr[first8], gr[pl.ds(8, 8)], gr[pl.ds(16, 8)]
    u2[18, 0, OWN] = gr[pl.ds(24, 32)]
    w1[18, 0, OWN] = gr[pl.ds(56, 32)]
    at = 0
    for ref, i, depth in ring:
        ref[33 - i, 0, top] = roll(above, at, 0)
        ref[33 - i, 0, low] = roll(below, -at, 0)
        at += depth
    for k in range(6):
        at = 0
        for ref, i, depth in ring:
            ref[33 - i, 1, pl.ds(8 * k, 8)] = roll(columns, -(at + depth + 16 * k), 1)
            at += 2 * depth

    lax.fori_loop(16, 18, first, 0)
    lax.fori_loop(15, 18, second, 0)
    lax.fori_loop(14, 17, finish, 0)

    for side in SIDES:
        @pl.when(has[side])
        def _():
            copies[side].wait_send()
    for side in far:
        @pl.when(has[side])
        def _():
            far[side].wait_send()
    zcopy.wait_send()
    gcopy.wait_send()


def solution(mesh):
    sizes = mesh.shape["gx"], mesh.shape["gy"]
    spec = P("gz", "gx", "gy")

    def body(log_range, sea_mask, forcing, cotangent):
        block = log_range.shape
        f32 = jnp.float32
        field = pltpu.VMEM((19, 2, 48, 128), f32)
        return pl.pallas_call(
            functools.partial(kernel, sizes),
            out_shape=[pltpu.VMEM(block, f32)] * 2,
            in_specs=[pl.BlockSpec(memory_space=pltpu.HBM)] * 4,
            out_specs=[pl.BlockSpec(memory_space=pltpu.VMEM)] * 2,
            scratch_shapes=[
                pltpu.VMEM(block, f32), pltpu.VMEM(block, jnp.int32), pltpu.VMEM(block, f32), pltpu.VMEM(block, f32),
                field, field, field, field, field, field, field,
                pltpu.VMEM((2, 16, 8, 128), f32), pltpu.VMEM((2, 16, 8, 128), f32),
                pltpu.VMEM((2, 32, 128), f32), pltpu.VMEM((2, 48, 128), f32),
                pltpu.VMEM((5, 32, 128), f32), pltpu.VMEM((5, 32, 128), f32),
                pltpu.VMEM((88, 128), f32), pltpu.VMEM((88, 128), f32),
                pltpu.SemaphoreType.DMA((4,)), pltpu.SemaphoreType.DMA((2, 12)),
                pltpu.SemaphoreType.REGULAR,
            ],
            compiler_params=pltpu.CompilerParams(collective_id=0, has_side_effects=True, vmem_limit_bytes=48 * 1024 * 1024),
            cost_estimate=pl.CostEstimate(flops=10_000_000, bytes_accessed=1_600_000, transcendentals=200_000),
        )(*(pltpu.with_memory_space_constraint(x, pltpu.HBM) for x in (log_range, sea_mask, forcing, cotangent)))

    def store(it, rg, it_h, rg_h, sem):
        copies = [pltpu.make_async_copy(v.at[pl.ds(16 * h, 16)], o.at[pl.ds(16 * h, 16)], sem.at[i, h])
                  for i, (v, o) in enumerate(((it, it_h), (rg, rg_h))) for h in range(1)]
        for copy in copies:
            copy.start()
        for copy in copies:
            copy.wait()

    def whole(*args):
        parts = body(*args)
        parts = [pltpu.with_memory_space_constraint(x, pltpu.VMEM) for x in parts]
        return pl.pallas_call(store, out_shape=[jax.ShapeDtypeStruct(x.shape, jnp.float32) for x in parts],
                              in_specs=[pl.BlockSpec(memory_space=pltpu.VMEM)] * 2,
                              out_specs=[pl.BlockSpec(memory_space=pl.ANY)] * 2,
                              scratch_shapes=[pltpu.SemaphoreType.DMA((2, 1))])(*parts)

    return jax.shard_map(whole, mesh=mesh, in_specs=(spec,) * 4, out_specs=(spec, spec), check_vma=False)
```

```python
import functools

import jax
import jax.numpy as jnp
from jax import lax
from jax.experimental import pallas as pl
from jax.experimental.pallas import tpu as pltpu
from jax.sharding import PartitionSpec as P

MESH = pl.DeviceIdType.MESH
SIDES = ((-1, -1), (1, -1), (-1, 1), (1, 1), (0, -1), (0, 1), (-1, 0), (1, 0))
RELAX = 0.9
KEEP = 1.0 - RELAX
TURNS = (0, 0, 0, 0, 0, 3, 2, 2)
LAND = RELAX * (1.0 + KEEP + KEEP * KEEP + KEEP * KEEP * KEEP)
OWN = pl.ds(8, 32)


def roll(value, shift, axis):
    size = value.shape[axis]
    shift = shift % size
    return pltpu.roll(value, shift, axis) if shift else value


def stencil_full(ref, i):
    lane = lax.broadcasted_iota(jnp.int32, (48, 128), 1)
    first, last = lane == 0, lane == 127
    c0, c1 = ref[i, 0], ref[i, 1]
    r0, r1 = roll(c0, 1, 1), roll(c1, 1, 1)
    l0, l1 = roll(c0, -1, 1), roll(c1, -1, 1)
    n0 = ref[i - 1, 0] + ref[i + 1, 0] + (roll(c0, 1, 0) + roll(c0, -1, 0))
    n1 = ref[i - 1, 1] + ref[i + 1, 1] + (roll(c1, 1, 0) + roll(c1, -1, 0))
    n0 = n0 + jnp.where(first, r1, r0) + jnp.where(last, l1, l0)
    n1 = n1 + jnp.where(first, r0, r1) + jnp.where(last, l0, l1)
    return (c0, c1), (n0, n1)


def stencil_own(ref, i):
    lane = lax.broadcasted_iota(jnp.int32, (32, 128), 1)
    c = ref[i, 0]
    own = c[8:40]
    side = ref[i, 1, OWN]
    n = ref[i - 1, 0, OWN] + ref[i + 1, 0, OWN]
    n = n + (roll(c, 1, 0)[8:40] + roll(c, -1, 0)[8:40])
    n = n + jnp.where(lane == 0, roll(side, 1, 1), roll(own, 1, 1))
    n = n + jnp.where(lane == 127, roll(side, -1, 1), roll(own, -1, 1))
    return own, n


def kernel(sizes, lr_h, m_h, f_h, c_h, it, rg,
           lr, ms, fo, co, a_, u1, u2, u3, w0, w1, w2,
           xs, xr, ys, yr, zs, zr, gs, gr, in_sem, sem, ready):
    nx, ny = sizes
    gz, gx, gy = lax.axis_index("gz"), lax.axis_index("gx"), lax.axis_index("gy")
    partner = {"gz": 1 - gz}
    has = {}
    for x, y in SIDES:
        here = []
        if x:
            here.append(gx > 0 if x < 0 else gx < nx - 1)
        if y:
            here.append(gy > 0 if y < 0 else gy < ny - 1)
        has[x, y] = here[0] if len(here) == 1 else here[0] & here[1]

    def at(side):
        return {"gx": gx + side[0], "gy": gy + side[1]}

    barrier = pltpu.get_barrier_semaphore()

    @pl.when(gz == 0)
    def _():
        pl.semaphore_signal(barrier, inc=1, device_id=partner, device_id_type=MESH)

    for side in SIDES:
        @pl.when(has[side])
        def _():
            pl.semaphore_signal(barrier, inc=1, device_id=at(side), device_id_type=MESH)

    loads = [pltpu.make_async_copy(h, v, in_sem.at[i]) for i, (h, v) in enumerate(((lr_h, lr), (m_h, ms), (f_h, fo), (c_h, co)))]
    for load in loads:
        load.start()

    def remote(src, dst, i, device):
        return pltpu.make_async_remote_copy(src_ref=src, dst_ref=dst, send_sem=sem.at[0, i], recv_sem=sem.at[1, i],
                                            device_id=device, device_id_type=MESH)

    low, mid, top = pl.ds(40, 8), pl.ds(8, 32), pl.ds(0, 8)
    first8, last8 = pl.ds(0, 8), pl.ds(24, 8)
    near, rest = pl.ds(13, 3), pl.ds(0, 13)
    copies = {}
    for i, (side, src, dst) in enumerate((
        ((-1, 0), xs.at[0, near], xr.at[0, near]), ((1, 0), xs.at[1, near], xr.at[1, near]),
        ((0, -1), ys.at[0], yr.at[0, mid]), ((0, 1), ys.at[1], yr.at[1, mid]),
        ((-1, -1), ys.at[0, first8], yr.at[0, low]), ((1, -1), ys.at[0, last8], yr.at[0, top]),
        ((-1, 1), ys.at[1, first8], yr.at[1, low]), ((1, 1), ys.at[1, last8], yr.at[1, top]),
    )):
        copies[side] = remote(src, dst, i, at(side))
    far = {side: remote(xs.at[i, rest], xr.at[i, rest], 10 + i, at(side)) for i, side in enumerate(SIDES[6:])}
    zcopy = remote(zs, zr, 8, partner)
    gcopy = remote(gs, gr, 9, partner)

    def source(i):
        return jnp.where(gz == 0, i, 15 - i)

    row8 = lax.broadcasted_iota(jnp.int32, (8, 128), 0)
    lane8 = lax.broadcasted_iota(jnp.int32, (8, 128), 1)
    lane32 = lax.broadcasted_iota(jnp.int32, (32, 128), 1)
    lane48 = lax.broadcasted_iota(jnp.int32, (48, 128), 1)
    zero = jnp.zeros((48, 128), jnp.float32)
    for ref in (u1, u2, u3, w0, w1, w2):
        ref[0, 0] = zero
        ref[0, 1] = zero
    for load in loads:
        load.wait()

    def prepare(i, carry):
        left, right = carry
        z = source(i)
        mask = ms[z].astype(jnp.float32)
        inverse = 1.0 / (mask * (6.0 + jnp.exp(-2.0 * lr[z])) + (1.0 - mask))
        weight = RELAX * mask * inverse
        u, w = weight * fo[z], weight * co[z]
        a_[i + 1, 0, OWN] = weight
        u1[i + 1, 0, OWN] = u
        w0[i + 1, 0, OWN] = w
        up_u, up_w, up_a = u[:8], w[:8], weight[:8]
        dn_u, dn_w, dn_a = u[24:], w[24:], weight[24:]
        xs[0, i] = jnp.where(row8 < 3, up_u, jnp.where(row8 < 6, roll(up_w, 3, 0), roll(up_a, 6, 0)))
        xs[1, i] = jnp.where(row8 >= 5, dn_u, jnp.where(row8 >= 2, roll(dn_w, -3, 0), roll(dn_a, -6, 0)))
        to_right = jnp.where(lane32 < 3, roll(u, 3, 1), jnp.where(lane32 < 6, roll(w, 6, 1), roll(weight, 8, 1)))
        to_left = jnp.where(lane32 < 3, u, jnp.where(lane32 < 6, roll(w, 3, 1), roll(weight, 6, 1)))
        left = jnp.where(lane32 < 8, to_left, roll(left, 8, 1))
        right = jnp.where(lane32 < 8, to_right, roll(right, 8, 1))
        return left, right

    left, right = lax.fori_loop(0, 16, prepare, (zero[:32], zero[:32]), unroll=2)
    ys[0] = left
    ys[1] = right
    for j, (ref, i) in enumerate(((u1, 16), (u1, 15), (w0, 16), (w0, 15), (a_, 16))):
        zs[j] = ref[i, 0, OWN]

    pl.semaphore_wait(barrier, gz + sum(h.astype(jnp.int32) for h in has.values()))

    @pl.when(gz == 1)
    def _():
        pl.semaphore_signal(ready, inc=1, device_id=partner, device_id_type=MESH)

    place = gx * 8 // nx
    turn = sum(jnp.where(place == i, t, 0) for i, t in enumerate(TURNS) if t)

    def send_layers(phase):
        @pl.when((gz == 1) & (turn == phase))
        def _():
            zcopy.start()
            if phase > 1:
                gcopy.start()

    for side in SIDES:
        @pl.when(has[side])
        def _():
            copies[side].start()
    send_layers(0)
    for side in far:
        @pl.when(has[side])
        def _():
            far[side].start()

    for side in SIDES:
        @pl.when(has[-side[0], -side[1]])
        def _():
            copies[side].wait_recv()
    send_layers(1)

    def halo(j, carry):
        left, right = carry
        i = 16 - j
        below = jnp.where(has[1, 0], xr[0, i - 1], 0.0)
        above = jnp.where(has[-1, 0], xr[1, i - 1], 0.0)
        u1[i, 0, low] = below
        w0[i, 0, low] = roll(below, -3, 0)
        a_[i, 0, low] = roll(below, -6, 0)
        u1[i, 0, top] = above
        w0[i, 0, top] = roll(above, 3, 0)
        a_[i, 0, top] = roll(above, 6, 0)
        half = lane48 < 64
        u1[i, 1] = jnp.where(half, right, roll(left, -3, 1))
        w0[i, 1] = jnp.where(half, roll(right, -3, 1), roll(left, -6, 1))
        a_[i, 1] = jnp.where(half, roll(right, -6, 1), roll(left, -8, 1))
        return roll(left, -8, 1), roll(right, -8, 1)

    def arrived(slot, y):
        parts = [jnp.where(has[x, y], yr[slot, rows], 0.0) for x, rows in ((-1, top), (0, mid), (1, low))]
        return jnp.concatenate(parts, axis=0)

    carry = lax.fori_loop(0, 3, halo, (arrived(1, -1), arrived(0, 1)), unroll=True)

    def sweep(old_u, new_u, old_w, new_w):
        def run(i, _):
            (c0, c1), (n0, n1) = stencil_full(old_u, i)
            new_u[i, 0] = KEEP * c0 + u1[i, 0] + a_[i, 0] * n0
            new_u[i, 1] = KEEP * c1 + u1[i, 1] + a_[i, 1] * n1
            (c0, c1), (n0, n1) = stencil_full(old_w, i)
            new_w[i, 0] = KEEP * c0 + a_[i, 0] * n0
            new_w[i, 1] = KEEP * c1 + a_[i, 1] * n1
            return 0
        return run

    def finish(i, _):
        z = source(i - 1)
        weight, s1 = a_[i, 0, OWN], u1[i, 0, OWN]
        c, n = stencil_own(u3, i)
        s4 = s1 + weight * n
        b, n = stencil_own(w2, i)
        w3 = KEEP * b + weight * n
        second = u2[i, 0, OWN]
        total = w0[i, 0, OWN] * s4 + w1[i, 0, OWN] * (c - KEEP * second) + b * (second - KEEP * s1) + w3 * s1
        rg[z] = (2.0 / RELAX) * jnp.exp(-2.0 * lr[z]) * total
        it[z] = jnp.where(ms[z] > 0, KEEP * c + s4, LAND * fo[z])
        return 0

    first = sweep(u1, u2, w0, w1)
    second = sweep(u2, u3, w1, w2)
    first(15, 0)
    ring = ((u1, 16, 2), (w0, 16, 2), (u1, 15, 1), (w0, 15, 1), (a_, 16, 1))
    above, below, columns = None, None, None
    at = 0
    for ref, i, depth in ring:
        t = roll(ref[i, 0, top], -at, 0)
        b = roll(ref[i, 0, low], at, 0)
        above = t if above is None else jnp.where(row8 < 8 - at, t, above)
        below = b if below is None else jnp.where(row8 >= at, b, below)
        at += depth
    for k in range(6):
        part, at = None, 0
        for ref, i, depth in ring:
            c = roll(ref[i, 1, pl.ds(8 * k, 8)], at + depth + 16 * k, 1)
            part = c if part is None else jnp.where(lane8 >= at + 16 * k, c, part)
            at += 2 * depth
        columns = part if columns is None else jnp.where(lane8 >= 16 * k, part, columns)
    gs[first8] = above
    gs[pl.ds(8, 8)] = below
    gs[pl.ds(16, 8)] = columns
    gs[pl.ds(24, 32)] = u2[15, 0, OWN]
    gs[pl.ds(56, 32)] = w1[15, 0, OWN]
    @pl.when((gz == 1) & (turn < 2))
    def _():
        gcopy.start()

    send_layers(2)

    for side in far:
        @pl.when(has[-side[0], -side[1]])
        def _():
            far[side].wait_recv()
    send_layers(3)
    lax.fori_loop(3, 16, halo, carry)
    lax.fori_loop(1, 6, first, 0, unroll=5)
    send_layers(4)
    lax.fori_loop(6, 15, first, 0, unroll=3)

    lax.fori_loop(1, 15, second, 0, unroll=2)
    @pl.when(gz == 0)
    def _():
        pl.semaphore_wait(ready, 1)
        zcopy.start()
        gcopy.start()
    lax.fori_loop(1, 14, finish, 0)

    zcopy.wait_recv()
    for j, (ref, i) in enumerate(((u1, 17), (u1, 18), (w0, 17), (w0, 18), (a_, 17))):
        ref[i, 0, OWN] = zr[j]
    gcopy.wait_recv()
    above, below, columns = gr[first8], gr[pl.ds(8, 8)], gr[pl.ds(16, 8)]
    u2[18, 0, OWN] = gr[pl.ds(24, 32)]
    w1[18, 0, OWN] = gr[pl.ds(56, 32)]
    at = 0
    for ref, i, depth in ring:
        ref[33 - i, 0, top] = roll(above, at, 0)
        ref[33 - i, 0, low] = roll(below, -at, 0)
        at += depth
    for k in range(6):
        at = 0
        for ref, i, depth in ring:
            ref[33 - i, 1, pl.ds(8 * k, 8)] = roll(columns, -(at + depth + 16 * k), 1)
            at += 2 * depth

    lax.fori_loop(16, 18, first, 0, unroll=True)
    lax.fori_loop(15, 18, second, 0, unroll=True)
    lax.fori_loop(14, 17, finish, 0, unroll=True)

    for side in SIDES:
        @pl.when(has[side])
        def _():
            copies[side].wait_send()
    for side in far:
        @pl.when(has[side])
        def _():
            far[side].wait_send()
    zcopy.wait_send()
    gcopy.wait_send()


def solution(mesh):
    sizes = mesh.shape["gx"], mesh.shape["gy"]
    spec = P("gz", "gx", "gy")

    def body(log_range, sea_mask, forcing, cotangent):
        block = log_range.shape
        f32 = jnp.float32
        field = pltpu.VMEM((19, 2, 48, 128), f32)
        return pl.pallas_call(
            functools.partial(kernel, sizes),
            out_shape=[pltpu.VMEM(block, f32)] * 2,
            in_specs=[pl.BlockSpec(memory_space=pltpu.HBM)] * 4,
            out_specs=[pl.BlockSpec(memory_space=pltpu.VMEM)] * 2,
            scratch_shapes=[
                pltpu.VMEM(block, f32), pltpu.VMEM(block, jnp.int32), pltpu.VMEM(block, f32), pltpu.VMEM(block, f32),
                field, field, field, field, field, field, field,
                pltpu.VMEM((2, 16, 8, 128), f32), pltpu.VMEM((2, 16, 8, 128), f32),
                pltpu.VMEM((2, 32, 128), f32), pltpu.VMEM((2, 48, 128), f32),
                pltpu.VMEM((5, 32, 128), f32), pltpu.VMEM((5, 32, 128), f32),
                pltpu.VMEM((88, 128), f32), pltpu.VMEM((88, 128), f32),
                pltpu.SemaphoreType.DMA((4,)), pltpu.SemaphoreType.DMA((2, 12)),
                pltpu.SemaphoreType.REGULAR,
            ],
            compiler_params=pltpu.CompilerParams(collective_id=0, has_side_effects=True, vmem_limit_bytes=48 * 1024 * 1024),
            cost_estimate=pl.CostEstimate(flops=10_000_000, bytes_accessed=1_600_000, transcendentals=200_000),
        )(*(pltpu.with_memory_space_constraint(x, pltpu.HBM) for x in (log_range, sea_mask, forcing, cotangent)))

    def store(it, rg, it_h, rg_h, sem):
        copies = [pltpu.make_async_copy(v.at[pl.ds(16 * h, 16)], o.at[pl.ds(16 * h, 16)], sem.at[i, h])
                  for i, (v, o) in enumerate(((it, it_h), (rg, rg_h))) for h in range(1)]
        for copy in copies:
            copy.start()
        for copy in copies:
            copy.wait()

    def whole(*args):
        parts = body(*args)
        parts = [pltpu.with_memory_space_constraint(x, pltpu.VMEM) for x in parts]
        return pl.pallas_call(store, out_shape=[jax.ShapeDtypeStruct(x.shape, jnp.float32) for x in parts],
                              in_specs=[pl.BlockSpec(memory_space=pltpu.VMEM)] * 2,
                              out_specs=[pl.BlockSpec(memory_space=pl.ANY)] * 2,
                              scratch_shapes=[pltpu.SemaphoreType.DMA((2, 1))])(*parts)

    return jax.shard_map(whole, mesh=mesh, in_specs=(spec,) * 4, out_specs=(spec, spec), check_vma=False)
```

```python
import functools

import jax
import jax.numpy as jnp
from jax import lax
from jax.experimental import pallas as pl
from jax.experimental.pallas import tpu as pltpu
from jax.sharding import PartitionSpec as P

MESH = pl.DeviceIdType.MESH
SIDES = ((-1, -1), (1, -1), (-1, 1), (1, 1), (0, -1), (0, 1), (-1, 0), (1, 0))
RELAX = 0.9
KEEP = 1.0 - RELAX
TURNS = (0, 0, 0, 0, 0, 3, 2, 2)
LAND = RELAX * (1.0 + KEEP + KEEP * KEEP + KEEP * KEEP * KEEP)
OWN = pl.ds(8, 32)


def roll(value, shift, axis):
    size = value.shape[axis]
    shift = shift % size
    return pltpu.roll(value, shift, axis) if shift else value


def stencil_full(ref, i):
    lane = lax.broadcasted_iota(jnp.int32, (48, 128), 1)
    first, last = lane == 0, lane == 127
    c0, c1 = ref[i, 0], ref[i, 1]
    r0, r1 = roll(c0, 1, 1), roll(c1, 1, 1)
    l0, l1 = roll(c0, -1, 1), roll(c1, -1, 1)
    n0 = ref[i - 1, 0] + ref[i + 1, 0] + (roll(c0, 1, 0) + roll(c0, -1, 0))
    n1 = ref[i - 1, 1] + ref[i + 1, 1] + (roll(c1, 1, 0) + roll(c1, -1, 0))
    n0 = n0 + jnp.where(first, r1, r0) + jnp.where(last, l1, l0)
    n1 = n1 + jnp.where(first, r0, r1) + jnp.where(last, l0, l1)
    return (c0, c1), (n0, n1)


def stencil_own(ref, i):
    lane = lax.broadcasted_iota(jnp.int32, (32, 128), 1)
    c = ref[i, 0]
    own = c[8:40]
    side = ref[i, 1, OWN]
    n = ref[i - 1, 0, OWN] + ref[i + 1, 0, OWN]
    n = n + (roll(c, 1, 0)[8:40] + roll(c, -1, 0)[8:40])
    n = n + jnp.where(lane == 0, roll(side, 1, 1), roll(own, 1, 1))
    n = n + jnp.where(lane == 127, roll(side, -1, 1), roll(own, -1, 1))
    return own, n


def last_step(i, z, lr, ms, fo, a_, u1, u2, u3, w0, w1, w2):
    weight, s1 = a_[i, 0, OWN], u1[i, 0, OWN]
    c, n = stencil_own(u3, i)
    s4 = s1 + weight * n
    b, n = stencil_own(w2, i)
    w3 = KEEP * b + weight * n
    second = u2[i, 0, OWN]
    total = w0[i, 0, OWN] * s4 + w1[i, 0, OWN] * (c - KEEP * second) + b * (second - KEEP * s1) + w3 * s1
    return jnp.where(ms[z] > 0, KEEP * c + s4, LAND * fo[z]), (2.0 / RELAX) * jnp.exp(-2.0 * lr[z]) * total


def kernel(sizes, lr_h, m_h, f_h, c_h, it, rg,
           lr, ms, fo, a_, u1, u2, u3, w0, w1, w2,
           co, xs, xr, ys, yr, zs, zr, gs, gr, in_sem, sem, ready):
    nx, ny = sizes
    gz, gx, gy = lax.axis_index("gz"), lax.axis_index("gx"), lax.axis_index("gy")
    partner = {"gz": 1 - gz}
    has = {}
    for x, y in SIDES:
        here = []
        if x:
            here.append(gx > 0 if x < 0 else gx < nx - 1)
        if y:
            here.append(gy > 0 if y < 0 else gy < ny - 1)
        has[x, y] = here[0] if len(here) == 1 else here[0] & here[1]

    def at(side):
        return {"gx": gx + side[0], "gy": gy + side[1]}

    barrier = pltpu.get_barrier_semaphore()

    @pl.when(gz == 0)
    def _():
        pl.semaphore_signal(barrier, inc=1, device_id=partner, device_id_type=MESH)

    for side in SIDES:
        @pl.when(has[side])
        def _():
            pl.semaphore_signal(barrier, inc=1, device_id=at(side), device_id_type=MESH)

    loads = [pltpu.make_async_copy(h, v, in_sem.at[i]) for i, (h, v) in enumerate(((lr_h, lr), (m_h, ms), (f_h, fo), (c_h, co)))]
    for load in loads:
        load.start()

    def remote(src, dst, i, device):
        return pltpu.make_async_remote_copy(src_ref=src, dst_ref=dst, send_sem=sem.at[0, i], recv_sem=sem.at[1, i],
                                            device_id=device, device_id_type=MESH)

    low, mid, top = pl.ds(40, 8), pl.ds(8, 32), pl.ds(0, 8)
    first8, last8 = pl.ds(0, 8), pl.ds(24, 8)
    near, rest = pl.ds(13, 3), pl.ds(0, 13)
    copies = {}
    for i, (side, src, dst) in enumerate((
        ((-1, 0), xs.at[0, near], xr.at[0, near]), ((1, 0), xs.at[1, near], xr.at[1, near]),
        ((0, -1), ys.at[0], yr.at[0, mid]), ((0, 1), ys.at[1], yr.at[1, mid]),
        ((-1, -1), ys.at[0, first8], yr.at[0, low]), ((1, -1), ys.at[0, last8], yr.at[0, top]),
        ((-1, 1), ys.at[1, first8], yr.at[1, low]), ((1, 1), ys.at[1, last8], yr.at[1, top]),
    )):
        copies[side] = remote(src, dst, i, at(side))
    far = {side: remote(xs.at[i, rest], xr.at[i, rest], 10 + i, at(side)) for i, side in enumerate(SIDES[6:])}
    zcopy = remote(zs, zr, 8, partner)
    gcopy = remote(gs, gr, 9, partner)

    def source(i):
        return jnp.where(gz == 0, i, 15 - i)

    row8 = lax.broadcasted_iota(jnp.int32, (8, 128), 0)
    lane8 = lax.broadcasted_iota(jnp.int32, (8, 128), 1)
    lane32 = lax.broadcasted_iota(jnp.int32, (32, 128), 1)
    lane48 = lax.broadcasted_iota(jnp.int32, (48, 128), 1)
    zero = jnp.zeros((48, 128), jnp.float32)
    for ref in (u1, u2, u3, w0, w1, w2):
        ref[0, 0] = zero
        ref[0, 1] = zero
    for load in loads:
        load.wait()

    def prepare(i, carry):
        left, right = carry
        z = source(i)
        mask = ms[z].astype(jnp.float32)
        inverse = 1.0 / (mask * (6.0 + jnp.exp(-2.0 * lr[z])) + (1.0 - mask))
        weight = RELAX * mask * inverse
        u, w = weight * fo[z], weight * co[z]
        a_[i + 1, 0, OWN] = weight
        u1[i + 1, 0, OWN] = u
        w0[i + 1, 0, OWN] = w
        up_u, up_w, up_a = u[:8], w[:8], weight[:8]
        dn_u, dn_w, dn_a = u[24:], w[24:], weight[24:]
        xs[0, i] = jnp.where(row8 < 3, up_u, jnp.where(row8 < 6, roll(up_w, 3, 0), roll(up_a, 6, 0)))
        xs[1, i] = jnp.where(row8 >= 5, dn_u, jnp.where(row8 >= 2, roll(dn_w, -3, 0), roll(dn_a, -6, 0)))
        to_right = jnp.where(lane32 < 3, roll(u, 3, 1), jnp.where(lane32 < 6, roll(w, 6, 1), roll(weight, 8, 1)))
        to_left = jnp.where(lane32 < 3, u, jnp.where(lane32 < 6, roll(w, 3, 1), roll(weight, 6, 1)))
        left = jnp.where(lane32 < 8, to_left, roll(left, 8, 1))
        right = jnp.where(lane32 < 8, to_right, roll(right, 8, 1))
        return left, right

    left, right = lax.fori_loop(0, 16, prepare, (zero[:32], zero[:32]), unroll=2)
    ys[0] = left
    ys[1] = right
    for j, (ref, i) in enumerate(((u1, 16), (u1, 15), (w0, 16), (w0, 15), (a_, 16))):
        zs[j] = ref[i, 0, OWN]

    pl.semaphore_wait(barrier, gz + sum(h.astype(jnp.int32) for h in has.values()))

    @pl.when(gz == 1)
    def _():
        pl.semaphore_signal(ready, inc=1, device_id=partner, device_id_type=MESH)

    place = gx * 8 // nx
    turn = sum(jnp.where(place == i, t, 0) for i, t in enumerate(TURNS) if t)

    def send_layers(phase):
        @pl.when((gz == 1) & (turn == phase))
        def _():
            zcopy.start()
            if phase > 1:
                gcopy.start()

    for side in SIDES:
        @pl.when(has[side])
        def _():
            copies[side].start()
    send_layers(0)
    for side in far:
        @pl.when(has[side])
        def _():
            far[side].start()

    for side in SIDES:
        @pl.when(has[-side[0], -side[1]])
        def _():
            copies[side].wait_recv()
    send_layers(1)

    def halo(j, carry):
        left, right = carry
        i = 16 - j
        below = jnp.where(has[1, 0], xr[0, i - 1], 0.0)
        above = jnp.where(has[-1, 0], xr[1, i - 1], 0.0)
        u1[i, 0, low] = below
        w0[i, 0, low] = roll(below, -3, 0)
        a_[i, 0, low] = roll(below, -6, 0)
        u1[i, 0, top] = above
        w0[i, 0, top] = roll(above, 3, 0)
        a_[i, 0, top] = roll(above, 6, 0)
        half = lane48 < 64
        u1[i, 1] = jnp.where(half, right, roll(left, -3, 1))
        w0[i, 1] = jnp.where(half, roll(right, -3, 1), roll(left, -6, 1))
        a_[i, 1] = jnp.where(half, roll(right, -6, 1), roll(left, -8, 1))
        return roll(left, -8, 1), roll(right, -8, 1)

    def arrived(slot, y):
        parts = [jnp.where(has[x, y], yr[slot, rows], 0.0) for x, rows in ((-1, top), (0, mid), (1, low))]
        return jnp.concatenate(parts, axis=0)

    carry = lax.fori_loop(0, 3, halo, (arrived(1, -1), arrived(0, 1)), unroll=True)

    def sweep(old_u, new_u, old_w, new_w):
        def run(i, _):
            (c0, c1), (n0, n1) = stencil_full(old_u, i)
            new_u[i, 0] = KEEP * c0 + u1[i, 0] + a_[i, 0] * n0
            new_u[i, 1] = KEEP * c1 + u1[i, 1] + a_[i, 1] * n1
            (c0, c1), (n0, n1) = stencil_full(old_w, i)
            new_w[i, 0] = KEEP * c0 + a_[i, 0] * n0
            new_w[i, 1] = KEEP * c1 + a_[i, 1] * n1
            return 0
        return run

    def finish(i, _):
        z = source(i - 1)
        it[z], rg[z] = last_step(i, z, lr, ms, fo, a_, u1, u2, u3, w0, w1, w2)
        return 0

    first = sweep(u1, u2, w0, w1)
    second = sweep(u2, u3, w1, w2)
    first(15, 0)
    ring = ((u1, 16, 2), (w0, 16, 2), (u1, 15, 1), (w0, 15, 1), (a_, 16, 1))
    above, below, columns = None, None, None
    at = 0
    for ref, i, depth in ring:
        t = roll(ref[i, 0, top], -at, 0)
        b = roll(ref[i, 0, low], at, 0)
        above = t if above is None else jnp.where(row8 < 8 - at, t, above)
        below = b if below is None else jnp.where(row8 >= at, b, below)
        at += depth
    for k in range(6):
        part, at = None, 0
        for ref, i, depth in ring:
            c = roll(ref[i, 1, pl.ds(8 * k, 8)], at + depth + 16 * k, 1)
            part = c if part is None else jnp.where(lane8 >= at + 16 * k, c, part)
            at += 2 * depth
        columns = part if columns is None else jnp.where(lane8 >= 16 * k, part, columns)
    gs[first8] = above
    gs[pl.ds(8, 8)] = below
    gs[pl.ds(16, 8)] = columns
    gs[pl.ds(24, 32)] = u2[15, 0, OWN]
    gs[pl.ds(56, 32)] = w1[15, 0, OWN]
    @pl.when((gz == 1) & (turn < 2))
    def _():
        gcopy.start()

    send_layers(2)

    for side in far:
        @pl.when(has[-side[0], -side[1]])
        def _():
            far[side].wait_recv()
    send_layers(3)
    lax.fori_loop(3, 16, halo, carry)
    lax.fori_loop(1, 6, first, 0, unroll=5)
    send_layers(4)
    lax.fori_loop(6, 15, first, 0, unroll=3)

    lax.fori_loop(1, 15, second, 0, unroll=2)
    @pl.when(gz == 0)
    def _():
        pl.semaphore_wait(ready, 1)
        zcopy.start()
        gcopy.start()
    lax.fori_loop(1, 14, finish, 0)

    zcopy.wait_recv()
    for j, (ref, i) in enumerate(((u1, 17), (u1, 18), (w0, 17), (w0, 18), (a_, 17))):
        ref[i, 0, OWN] = zr[j]
    gcopy.wait_recv()
    above, below, columns = gr[first8], gr[pl.ds(8, 8)], gr[pl.ds(16, 8)]
    u2[18, 0, OWN] = gr[pl.ds(24, 32)]
    w1[18, 0, OWN] = gr[pl.ds(56, 32)]
    at = 0
    for ref, i, depth in ring:
        ref[33 - i, 0, top] = roll(above, at, 0)
        ref[33 - i, 0, low] = roll(below, -at, 0)
        at += depth
    for k in range(6):
        at = 0
        for ref, i, depth in ring:
            ref[33 - i, 1, pl.ds(8 * k, 8)] = roll(columns, -(at + depth + 16 * k), 1)
            at += 2 * depth

    lax.fori_loop(16, 18, first, 0, unroll=True)
    lax.fori_loop(15, 18, second, 0, unroll=True)

    for side in SIDES:
        @pl.when(has[side])
        def _():
            copies[side].wait_send()
    for side in far:
        @pl.when(has[side])
        def _():
            far[side].wait_send()
    zcopy.wait_send()
    gcopy.wait_send()


def solution(mesh):
    sizes = mesh.shape["gx"], mesh.shape["gy"]
    spec = P("gz", "gx", "gy")

    def body(log_range, sea_mask, forcing, cotangent):
        block = log_range.shape
        f32 = jnp.float32
        field = pltpu.VMEM((19, 2, 48, 128), f32)
        return pl.pallas_call(
            functools.partial(kernel, sizes),
            out_shape=[pltpu.VMEM(block, f32)] * 3 + [pltpu.VMEM(block, jnp.int32), pltpu.VMEM(block, f32)] + [field] * 7,
            in_specs=[pl.BlockSpec(memory_space=pltpu.HBM)] * 4,
            out_specs=[pl.BlockSpec(memory_space=pltpu.VMEM)] * 12,
            scratch_shapes=[
                pltpu.VMEM(block, f32),
                pltpu.VMEM((2, 16, 8, 128), f32), pltpu.VMEM((2, 16, 8, 128), f32),
                pltpu.VMEM((2, 32, 128), f32), pltpu.VMEM((2, 48, 128), f32),
                pltpu.VMEM((5, 32, 128), f32), pltpu.VMEM((5, 32, 128), f32),
                pltpu.VMEM((88, 128), f32), pltpu.VMEM((88, 128), f32),
                pltpu.SemaphoreType.DMA((4,)), pltpu.SemaphoreType.DMA((2, 12)),
                pltpu.SemaphoreType.REGULAR,
            ],
            compiler_params=pltpu.CompilerParams(collective_id=0, has_side_effects=True, vmem_limit_bytes=16 * 1024 * 1024),
            cost_estimate=pl.CostEstimate(flops=10_000_000, bytes_accessed=1_600_000, transcendentals=200_000),
        )(*(pltpu.with_memory_space_constraint(x, pltpu.HBM) for x in (log_range, sea_mask, forcing, cotangent)))

    def store(it, rg, lr, ms, fo, a_, u1, u2, u3, w0, w1, w2, it_h, rg_h, last_it, last_rg, sem):
        gz = lax.axis_index("gz")
        bulk, start = pl.ds(3 * gz, 13), 13 * (1 - gz)
        copies = [pltpu.make_async_copy(v, h, sem.at[i]) for i, (v, h) in enumerate((
            (it.at[bulk], it_h.at[bulk]), (rg.at[bulk], rg_h.at[bulk]),
            (last_it, it_h.at[pl.ds(start, 3)]), (last_rg, rg_h.at[pl.ds(start, 3)])))]
        copies[0].start()
        copies[1].start()
        for i in range(14, 17):
            z = jnp.where(gz == 0, i - 1, 16 - i)
            last_it[z - start], last_rg[z - start] = last_step(i, z, lr, ms, fo, a_, u1, u2, u3, w0, w1, w2)
        copies[2].start()
        copies[3].start()
        for copy in copies:
            copy.wait()

    def whole(*args):
        parts = [pltpu.with_memory_space_constraint(x, pltpu.VMEM) for x in body(*args)]
        block = parts[0].shape
        last = pltpu.VMEM((3, *block[1:]), jnp.float32)
        return pl.pallas_call(store, out_shape=[jax.ShapeDtypeStruct(block, jnp.float32)] * 2,
                              in_specs=[pl.BlockSpec(memory_space=pltpu.VMEM)] * 12,
                              out_specs=[pl.BlockSpec(memory_space=pl.ANY)] * 2,
                              scratch_shapes=[last, last, pltpu.SemaphoreType.DMA((4,))],
                              compiler_params=pltpu.CompilerParams(vmem_limit_bytes=4 * 1024 * 1024))(*parts)

    return jax.shard_map(whole, mesh=mesh, in_specs=(spec,) * 4, out_specs=(spec, spec), check_vma=False)
```

```python
import functools

import jax
import jax.numpy as jnp
from jax import lax
from jax.experimental import pallas as pl
from jax.experimental.pallas import tpu as pltpu
from jax.sharding import PartitionSpec as P

MESH = pl.DeviceIdType.MESH
SIDES = ((-1, -1), (1, -1), (-1, 1), (1, 1), (0, -1), (0, 1), (-1, 0), (1, 0))
RELAX = 0.9
KEEP = 1.0 - RELAX
TURNS = (0, 0, 0, 0, 0, 2, 2, 2)
LAND = RELAX * (1.0 + KEEP + KEEP * KEEP + KEEP * KEEP * KEEP)
OWN = pl.ds(8, 32)


def roll(value, shift, axis):
    size = value.shape[axis]
    shift = shift % size
    return pltpu.roll(value, shift, axis) if shift else value


def stencil_full(ref, i):
    lane = lax.broadcasted_iota(jnp.int32, (48, 128), 1)
    first, last = lane == 0, lane == 127
    c0, c1 = ref[i, 0], ref[i, 1]
    r0, r1 = roll(c0, 1, 1), roll(c1, 1, 1)
    l0, l1 = roll(c0, -1, 1), roll(c1, -1, 1)
    n0 = ref[i - 1, 0] + ref[i + 1, 0] + (roll(c0, 1, 0) + roll(c0, -1, 0))
    n1 = ref[i - 1, 1] + ref[i + 1, 1] + (roll(c1, 1, 0) + roll(c1, -1, 0))
    n0 = n0 + jnp.where(first, r1, r0) + jnp.where(last, l1, l0)
    n1 = n1 + jnp.where(first, r0, r1) + jnp.where(last, l0, l1)
    return (c0, c1), (n0, n1)


def stencil_own(ref, i):
    lane = lax.broadcasted_iota(jnp.int32, (32, 128), 1)
    c = ref[i, 0]
    own = c[8:40]
    side = ref[i, 1, OWN]
    n = ref[i - 1, 0, OWN] + ref[i + 1, 0, OWN]
    n = n + (roll(c, 1, 0)[8:40] + roll(c, -1, 0)[8:40])
    n = n + jnp.where(lane == 0, roll(side, 1, 1), roll(own, 1, 1))
    n = n + jnp.where(lane == 127, roll(side, -1, 1), roll(own, -1, 1))
    return own, n


def kernel(sizes, lr_h, m_h, f_h, c_h, it, rg,
           lr, ms, fo, co, a_, u1, u2, u3, w0, w1, w2,
           xs, xr, ys, yr, zs, zr, gs, gr, in_sem, sem, ready):
    nx, ny = sizes
    gz, gx, gy = lax.axis_index("gz"), lax.axis_index("gx"), lax.axis_index("gy")
    partner = {"gz": 1 - gz}
    has = {}
    for x, y in SIDES:
        here = []
        if x:
            here.append(gx > 0 if x < 0 else gx < nx - 1)
        if y:
            here.append(gy > 0 if y < 0 else gy < ny - 1)
        has[x, y] = here[0] if len(here) == 1 else here[0] & here[1]

    def at(side):
        return {"gx": gx + side[0], "gy": gy + side[1]}

    barrier = pltpu.get_barrier_semaphore()

    @pl.when(gz == 0)
    def _():
        pl.semaphore_signal(barrier, inc=1, device_id=partner, device_id_type=MESH)

    for side in SIDES:
        @pl.when(has[side])
        def _():
            pl.semaphore_signal(barrier, inc=1, device_id=at(side), device_id_type=MESH)

    loads = [pltpu.make_async_copy(h, v, in_sem.at[i]) for i, (h, v) in enumerate(((lr_h, lr), (m_h, ms), (f_h, fo), (c_h, co)))]
    for load in loads:
        load.start()

    def remote(src, dst, i, device):
        return pltpu.make_async_remote_copy(src_ref=src, dst_ref=dst, send_sem=sem.at[0, i], recv_sem=sem.at[1, i],
                                            device_id=device, device_id_type=MESH)

    low, mid, top = pl.ds(40, 8), pl.ds(8, 32), pl.ds(0, 8)
    first8, last8 = pl.ds(0, 8), pl.ds(24, 8)
    near, rest = pl.ds(13, 3), pl.ds(0, 13)
    copies = {}
    for i, (side, src, dst) in enumerate((
        ((-1, 0), xs.at[0, near], xr.at[0, near]), ((1, 0), xs.at[1, near], xr.at[1, near]),
        ((0, -1), ys.at[0], yr.at[0, mid]), ((0, 1), ys.at[1], yr.at[1, mid]),
        ((-1, -1), ys.at[0, first8], yr.at[0, low]), ((1, -1), ys.at[0, last8], yr.at[0, top]),
        ((-1, 1), ys.at[1, first8], yr.at[1, low]), ((1, 1), ys.at[1, last8], yr.at[1, top]),
    )):
        copies[side] = remote(src, dst, i, at(side))
    far = {side: remote(xs.at[i, rest], xr.at[i, rest], 10 + i, at(side)) for i, side in enumerate(SIDES[6:])}
    zcopy = remote(zs, zr, 8, partner)
    gcopy = remote(gs, gr, 9, partner)

    def source(i):
        return jnp.where(gz == 0, i, 15 - i)

    row8 = lax.broadcasted_iota(jnp.int32, (8, 128), 0)
    lane8 = lax.broadcasted_iota(jnp.int32, (8, 128), 1)
    lane32 = lax.broadcasted_iota(jnp.int32, (32, 128), 1)
    lane48 = lax.broadcasted_iota(jnp.int32, (48, 128), 1)
    zero = jnp.zeros((48, 128), jnp.float32)
    for ref in (u1, u2, u3, w0, w1, w2):
        ref[0, 0] = zero
        ref[0, 1] = zero
    for load in loads:
        load.wait()

    def prepare(i, carry):
        left, right = carry
        z = source(i)
        mask = ms[z].astype(jnp.float32)
        inverse = 1.0 / (mask * (6.0 + jnp.exp(-2.0 * lr[z])) + (1.0 - mask))
        weight = RELAX * mask * inverse
        u, w = weight * fo[z], weight * co[z]
        a_[i + 1, 0, OWN] = weight
        u1[i + 1, 0, OWN] = u
        w0[i + 1, 0, OWN] = w
        up_u, up_w, up_a = u[:8], w[:8], weight[:8]
        dn_u, dn_w, dn_a = u[24:], w[24:], weight[24:]
        xs[0, i] = jnp.where(row8 < 3, up_u, jnp.where(row8 < 6, roll(up_w, 3, 0), roll(up_a, 6, 0)))
        xs[1, i] = jnp.where(row8 >= 5, dn_u, jnp.where(row8 >= 2, roll(dn_w, -3, 0), roll(dn_a, -6, 0)))
        to_right = jnp.where(lane32 < 3, roll(u, 3, 1), jnp.where(lane32 < 6, roll(w, 6, 1), roll(weight, 8, 1)))
        to_left = jnp.where(lane32 < 3, u, jnp.where(lane32 < 6, roll(w, 3, 1), roll(weight, 6, 1)))
        left = jnp.where(lane32 < 8, to_left, roll(left, 8, 1))
        right = jnp.where(lane32 < 8, to_right, roll(right, 8, 1))
        return left, right

    left, right = lax.fori_loop(0, 16, prepare, (zero[:32], zero[:32]), unroll=2)
    ys[0] = left
    ys[1] = right
    for j, (ref, i) in enumerate(((u1, 16), (u1, 15), (w0, 16), (w0, 15), (a_, 16))):
        zs[j] = ref[i, 0, OWN]

    pl.semaphore_wait(barrier, gz + sum(h.astype(jnp.int32) for h in has.values()))

    @pl.when(gz == 1)
    def _():
        pl.semaphore_signal(ready, inc=1, device_id=partner, device_id_type=MESH)

    place = gx * 8 // nx
    turn = sum(jnp.where(place == i, t, 0) for i, t in enumerate(TURNS) if t)

    def send_layers(phase):
        @pl.when((gz == 1) & (turn == phase))
        def _():
            zcopy.start()
            if phase > 1:
                gcopy.start()

    for side in SIDES:
        @pl.when(has[side])
        def _():
            copies[side].start()
    send_layers(0)
    for side in far:
        @pl.when(has[side] & (gz == 0))
        def _():
            far[side].start()

    for side in SIDES:
        @pl.when(has[-side[0], -side[1]])
        def _():
            copies[side].wait_recv()
    send_layers(1)

    def halo(j, carry):
        left, right = carry
        i = 16 - j
        below = jnp.where(has[1, 0], xr[0, i - 1], 0.0)
        above = jnp.where(has[-1, 0], xr[1, i - 1], 0.0)
        u1[i, 0, low] = below
        w0[i, 0, low] = roll(below, -3, 0)
        a_[i, 0, low] = roll(below, -6, 0)
        u1[i, 0, top] = above
        w0[i, 0, top] = roll(above, 3, 0)
        a_[i, 0, top] = roll(above, 6, 0)
        half = lane48 < 64
        u1[i, 1] = jnp.where(half, right, roll(left, -3, 1))
        w0[i, 1] = jnp.where(half, roll(right, -3, 1), roll(left, -6, 1))
        a_[i, 1] = jnp.where(half, roll(right, -6, 1), roll(left, -8, 1))
        return roll(left, -8, 1), roll(right, -8, 1)

    def arrived(slot, y):
        parts = [jnp.where(has[x, y], yr[slot, rows], 0.0) for x, rows in ((-1, top), (0, mid), (1, low))]
        return jnp.concatenate(parts, axis=0)

    carry = lax.fori_loop(0, 3, halo, (arrived(1, -1), arrived(0, 1)), unroll=True)

    def sweep(old_u, new_u, old_w, new_w):
        def run(i, _):
            (c0, c1), (n0, n1) = stencil_full(old_u, i)
            new_u[i, 0] = KEEP * c0 + u1[i, 0] + a_[i, 0] * n0
            new_u[i, 1] = KEEP * c1 + u1[i, 1] + a_[i, 1] * n1
            (c0, c1), (n0, n1) = stencil_full(old_w, i)
            new_w[i, 0] = KEEP * c0 + a_[i, 0] * n0
            new_w[i, 1] = KEEP * c1 + a_[i, 1] * n1
            return 0
        return run

    def finish(i, _):
        z = source(i - 1)
        weight, s1 = a_[i, 0, OWN], u1[i, 0, OWN]
        c, n = stencil_own(u3, i)
        s4 = s1 + weight * n
        b, n = stencil_own(w2, i)
        w3 = KEEP * b + weight * n
        second = u2[i, 0, OWN]
        total = w0[i, 0, OWN] * s4 + w1[i, 0, OWN] * (c - KEEP * second) + b * (second - KEEP * s1) + w3 * s1
        rg[z] = (2.0 / RELAX) * jnp.exp(-2.0 * lr[z]) * total
        it[z] = jnp.where(ms[z] > 0, KEEP * c + s4, LAND * fo[z])
        return 0

    first = sweep(u1, u2, w0, w1)
    second = sweep(u2, u3, w1, w2)
    first(15, 0)
    ring = ((u1, 16, 2), (w0, 16, 2), (u1, 15, 1), (w0, 15, 1), (a_, 16, 1))
    above, below, columns = None, None, None
    at = 0
    for ref, i, depth in ring:
        t = roll(ref[i, 0, top], -at, 0)
        b = roll(ref[i, 0, low], at, 0)
        above = t if above is None else jnp.where(row8 < 8 - at, t, above)
        below = b if below is None else jnp.where(row8 >= at, b, below)
        at += depth
    for k in range(6):
        part, at = None, 0
        for ref, i, depth in ring:
            c = roll(ref[i, 1, pl.ds(8 * k, 8)], at + depth + 16 * k, 1)
            part = c if part is None else jnp.where(lane8 >= at + 16 * k, c, part)
            at += 2 * depth
        columns = part if columns is None else jnp.where(lane8 >= 16 * k, part, columns)
    gs[first8] = above
    gs[pl.ds(8, 8)] = below
    gs[pl.ds(16, 8)] = columns
    gs[pl.ds(24, 32)] = u2[15, 0, OWN]
    gs[pl.ds(56, 32)] = w1[15, 0, OWN]
    @pl.when((gz == 1) & (turn < 2))
    def _():
        gcopy.start()

    send_layers(2)

    for side in far:
        @pl.when(has[side] & (gz == 1))
        def _():
            far[side].start()
    send_layers(3)
    for side in far:
        @pl.when(has[-side[0], -side[1]])
        def _():
            far[side].wait_recv()
    lax.fori_loop(3, 16, halo, carry)
    lax.fori_loop(1, 6, first, 0, unroll=5)
    send_layers(4)
    lax.fori_loop(6, 15, first, 0, unroll=3)

    lax.fori_loop(1, 15, second, 0, unroll=2)
    @pl.when(gz == 0)
    def _():
        pl.semaphore_wait(ready, 1)
        zcopy.start()
        gcopy.start()
    lax.fori_loop(1, 14, finish, 0)

    zcopy.wait_recv()
    for j, (ref, i) in enumerate(((u1, 17), (u1, 18), (w0, 17), (w0, 18), (a_, 17))):
        ref[i, 0, OWN] = zr[j]
    gcopy.wait_recv()
    above, below, columns = gr[first8], gr[pl.ds(8, 8)], gr[pl.ds(16, 8)]
    u2[18, 0, OWN] = gr[pl.ds(24, 32)]
    w1[18, 0, OWN] = gr[pl.ds(56, 32)]
    at = 0
    for ref, i, depth in ring:
        ref[33 - i, 0, top] = roll(above, at, 0)
        ref[33 - i, 0, low] = roll(below, -at, 0)
        at += depth
    for k in range(6):
        at = 0
        for ref, i, depth in ring:
            ref[33 - i, 1, pl.ds(8 * k, 8)] = roll(columns, -(at + depth + 16 * k), 1)
            at += 2 * depth

    lax.fori_loop(16, 18, first, 0, unroll=True)
    lax.fori_loop(15, 18, second, 0, unroll=True)
    lax.fori_loop(14, 17, finish, 0, unroll=True)

    for side in SIDES:
        @pl.when(has[side])
        def _():
            copies[side].wait_send()
    for side in far:
        @pl.when(has[side])
        def _():
            far[side].wait_send()
    zcopy.wait_send()
    gcopy.wait_send()


def solution(mesh):
    sizes = mesh.shape["gx"], mesh.shape["gy"]
    spec = P("gz", "gx", "gy")

    def body(log_range, sea_mask, forcing, cotangent):
        block = log_range.shape
        f32 = jnp.float32
        field = pltpu.VMEM((19, 2, 48, 128), f32)
        return pl.pallas_call(
            functools.partial(kernel, sizes),
            out_shape=[pltpu.VMEM(block, f32)] * 2,
            in_specs=[pl.BlockSpec(memory_space=pltpu.HBM)] * 4,
            out_specs=[pl.BlockSpec(memory_space=pltpu.VMEM)] * 2,
            scratch_shapes=[
                pltpu.VMEM(block, f32), pltpu.VMEM(block, jnp.int32), pltpu.VMEM(block, f32), pltpu.VMEM(block, f32),
                field, field, field, field, field, field, field,
                pltpu.VMEM((2, 16, 8, 128), f32), pltpu.VMEM((2, 16, 8, 128), f32),
                pltpu.VMEM((2, 32, 128), f32), pltpu.VMEM((2, 48, 128), f32),
                pltpu.VMEM((5, 32, 128), f32), pltpu.VMEM((5, 32, 128), f32),
                pltpu.VMEM((88, 128), f32), pltpu.VMEM((88, 128), f32),
                pltpu.SemaphoreType.DMA((4,)), pltpu.SemaphoreType.DMA((2, 12)),
                pltpu.SemaphoreType.REGULAR,
            ],
            compiler_params=pltpu.CompilerParams(collective_id=0, has_side_effects=True, vmem_limit_bytes=48 * 1024 * 1024),
            cost_estimate=pl.CostEstimate(flops=10_000_000, bytes_accessed=1_600_000, transcendentals=200_000),
        )(*(pltpu.with_memory_space_constraint(x, pltpu.HBM) for x in (log_range, sea_mask, forcing, cotangent)))

    def store(it, rg, it_h, rg_h, sem):
        copies = [pltpu.make_async_copy(v.at[pl.ds(16 * h, 16)], o.at[pl.ds(16 * h, 16)], sem.at[i, h])
                  for i, (v, o) in enumerate(((it, it_h), (rg, rg_h))) for h in range(1)]
        for copy in copies:
            copy.start()
        for copy in copies:
            copy.wait()

    def whole(*args):
        parts = body(*args)
        parts = [pltpu.with_memory_space_constraint(x, pltpu.VMEM) for x in parts]
        return pl.pallas_call(store, out_shape=[jax.ShapeDtypeStruct(x.shape, jnp.float32) for x in parts],
                              in_specs=[pl.BlockSpec(memory_space=pltpu.VMEM)] * 2,
                              out_specs=[pl.BlockSpec(memory_space=pl.ANY)] * 2,
                              scratch_shapes=[pltpu.SemaphoreType.DMA((2, 1))])(*parts)

    return jax.shard_map(whole, mesh=mesh, in_specs=(spec,) * 4, out_specs=(spec, spec), check_vma=False)
```

```python
import functools

import jax
import jax.numpy as jnp
from jax import lax
from jax.experimental import pallas as pl
from jax.experimental.pallas import tpu as pltpu
from jax.sharding import PartitionSpec as P

MESH = pl.DeviceIdType.MESH
SIDES = ((-1, -1), (1, -1), (-1, 1), (1, 1), (0, -1), (0, 1), (-1, 0), (1, 0))
RELAX = 0.9
KEEP = 1.0 - RELAX
TURNS = (0, 0, 0, 0, 0, 2, 2, 2)
LAND = RELAX * (1.0 + KEEP + KEEP * KEEP + KEEP * KEEP * KEEP)
OWN = pl.ds(8, 32)


def roll(value, shift, axis):
    size = value.shape[axis]
    shift = shift % size
    return pltpu.roll(value, shift, axis) if shift else value


def stencil_full(ref, i):
    lane = lax.broadcasted_iota(jnp.int32, (48, 128), 1)
    first, last = lane == 0, lane == 127
    c0, c1 = ref[i, 0], ref[i, 1]
    r0, r1 = roll(c0, 1, 1), roll(c1, 1, 1)
    l0, l1 = roll(c0, -1, 1), roll(c1, -1, 1)
    n0 = ref[i - 1, 0] + ref[i + 1, 0] + (roll(c0, 1, 0) + roll(c0, -1, 0))
    n1 = ref[i - 1, 1] + ref[i + 1, 1] + (roll(c1, 1, 0) + roll(c1, -1, 0))
    n0 = n0 + jnp.where(first, r1, r0) + jnp.where(last, l1, l0)
    n1 = n1 + jnp.where(first, r0, r1) + jnp.where(last, l0, l1)
    return (c0, c1), (n0, n1)


def stencil_own(ref, i):
    lane = lax.broadcasted_iota(jnp.int32, (32, 128), 1)
    c = ref[i, 0]
    own = c[8:40]
    side = ref[i, 1, OWN]
    n = ref[i - 1, 0, OWN] + ref[i + 1, 0, OWN]
    n = n + (roll(c, 1, 0)[8:40] + roll(c, -1, 0)[8:40])
    n = n + jnp.where(lane == 0, roll(side, 1, 1), roll(own, 1, 1))
    n = n + jnp.where(lane == 127, roll(side, -1, 1), roll(own, -1, 1))
    return own, n


def kernel(sizes, lr_h, m_h, f_h, c_h, it, rg,
           lr, ms, fo, co, a_, u1, u2, u3, w0, w1, w2,
           xs, xr, ys, yr, zs, zr, gs, gr, in_sem, sem, ready):
    nx, ny = sizes
    gz, gx, gy = lax.axis_index("gz"), lax.axis_index("gx"), lax.axis_index("gy")
    partner = {"gz": 1 - gz}
    has = {}
    for x, y in SIDES:
        here = []
        if x:
            here.append(gx > 0 if x < 0 else gx < nx - 1)
        if y:
            here.append(gy > 0 if y < 0 else gy < ny - 1)
        has[x, y] = here[0] if len(here) == 1 else here[0] & here[1]

    def at(side):
        return {"gx": gx + side[0], "gy": gy + side[1]}

    barrier = pltpu.get_barrier_semaphore()

    @pl.when(gz == 0)
    def _():
        pl.semaphore_signal(barrier, inc=1, device_id=partner, device_id_type=MESH)

    for side in SIDES:
        @pl.when(has[side])
        def _():
            pl.semaphore_signal(barrier, inc=1, device_id=at(side), device_id_type=MESH)

    loads = [pltpu.make_async_copy(h, v, in_sem.at[i]) for i, (h, v) in enumerate(((lr_h, lr), (m_h, ms), (f_h, fo), (c_h, co)))]
    for load in loads:
        load.start()

    def remote(src, dst, i, device):
        return pltpu.make_async_remote_copy(src_ref=src, dst_ref=dst, send_sem=sem.at[0, i], recv_sem=sem.at[1, i],
                                            device_id=device, device_id_type=MESH)

    low, mid, top = pl.ds(40, 8), pl.ds(8, 32), pl.ds(0, 8)
    first8, last8 = pl.ds(0, 8), pl.ds(24, 8)
    near, rest = pl.ds(13, 3), pl.ds(0, 13)
    copies = {}
    for i, (side, src, dst) in enumerate((
        ((-1, 0), xs.at[0, near], xr.at[0, near]), ((1, 0), xs.at[1, near], xr.at[1, near]),
        ((0, -1), ys.at[0], yr.at[0, mid]), ((0, 1), ys.at[1], yr.at[1, mid]),
        ((-1, -1), ys.at[0, first8], yr.at[0, low]), ((1, -1), ys.at[0, last8], yr.at[0, top]),
        ((-1, 1), ys.at[1, first8], yr.at[1, low]), ((1, 1), ys.at[1, last8], yr.at[1, top]),
    )):
        copies[side] = remote(src, dst, i, at(side))
    far = {side: remote(xs.at[i, rest], xr.at[i, rest], 10 + i, at(side)) for i, side in enumerate(SIDES[6:])}
    zcopy = remote(zs, zr, 8, partner)
    gcopy = remote(gs, gr, 9, partner)

    def source(i):
        return jnp.where(gz == 0, i, 15 - i)

    row8 = lax.broadcasted_iota(jnp.int32, (8, 128), 0)
    lane8 = lax.broadcasted_iota(jnp.int32, (8, 128), 1)
    lane32 = lax.broadcasted_iota(jnp.int32, (32, 128), 1)
    lane48 = lax.broadcasted_iota(jnp.int32, (48, 128), 1)
    zero = jnp.zeros((48, 128), jnp.float32)
    for ref in (u1, u2, u3, w0, w1, w2):
        ref[0, 0] = zero
        ref[0, 1] = zero
    for load in loads:
        load.wait()

    def prepare(i, carry):
        left, right = carry
        z = source(i)
        mask = ms[z].astype(jnp.float32)
        inverse = 1.0 / (mask * (6.0 + jnp.exp(-2.0 * lr[z])) + (1.0 - mask))
        weight = RELAX * mask * inverse
        u, w = weight * fo[z], weight * co[z]
        a_[i + 1, 0, OWN] = weight
        u1[i + 1, 0, OWN] = u
        w0[i + 1, 0, OWN] = w
        up_u, up_w, up_a = u[:8], w[:8], weight[:8]
        dn_u, dn_w, dn_a = u[24:], w[24:], weight[24:]
        xs[0, i] = jnp.where(row8 < 3, up_u, jnp.where(row8 < 6, roll(up_w, 3, 0), roll(up_a, 6, 0)))
        xs[1, i] = jnp.where(row8 >= 5, dn_u, jnp.where(row8 >= 2, roll(dn_w, -3, 0), roll(dn_a, -6, 0)))
        to_right = jnp.where(lane32 < 3, roll(u, 3, 1), jnp.where(lane32 < 6, roll(w, 6, 1), roll(weight, 8, 1)))
        to_left = jnp.where(lane32 < 3, u, jnp.where(lane32 < 6, roll(w, 3, 1), roll(weight, 6, 1)))
        left = jnp.where(lane32 < 8, to_left, roll(left, 8, 1))
        right = jnp.where(lane32 < 8, to_right, roll(right, 8, 1))
        return left, right

    left, right = lax.fori_loop(0, 16, prepare, (zero[:32], zero[:32]), unroll=2)
    ys[0] = left
    ys[1] = right
    for j, (ref, i) in enumerate(((u1, 16), (u1, 15), (w0, 16), (w0, 15), (a_, 16))):
        zs[j] = ref[i, 0, OWN]

    pl.semaphore_wait(barrier, gz + sum(h.astype(jnp.int32) for h in has.values()))

    @pl.when(gz == 1)
    def _():
        pl.semaphore_signal(ready, inc=1, device_id=partner, device_id_type=MESH)

    place = gx * 8 // nx
    turn = sum(jnp.where(place == i, t, 0) for i, t in enumerate(TURNS) if t)

    def send_layers(phase):
        @pl.when((gz == 1) & (turn == phase))
        def _():
            zcopy.start()
            if phase > 1:
                gcopy.start()

    for side in SIDES:
        @pl.when(has[side])
        def _():
            copies[side].start()
    send_layers(0)
    for side in far:
        @pl.when(has[side] & ((gz == 0) | (place > 2)))
        def _():
            far[side].start()

    for side in SIDES:
        @pl.when(has[-side[0], -side[1]])
        def _():
            copies[side].wait_recv()
    send_layers(1)

    def halo(j, carry):
        left, right = carry
        i = 16 - j
        below = jnp.where(has[1, 0], xr[0, i - 1], 0.0)
        above = jnp.where(has[-1, 0], xr[1, i - 1], 0.0)
        u1[i, 0, low] = below
        w0[i, 0, low] = roll(below, -3, 0)
        a_[i, 0, low] = roll(below, -6, 0)
        u1[i, 0, top] = above
        w0[i, 0, top] = roll(above, 3, 0)
        a_[i, 0, top] = roll(above, 6, 0)
        half = lane48 < 64
        u1[i, 1] = jnp.where(half, right, roll(left, -3, 1))
        w0[i, 1] = jnp.where(half, roll(right, -3, 1), roll(left, -6, 1))
        a_[i, 1] = jnp.where(half, roll(right, -6, 1), roll(left, -8, 1))
        return roll(left, -8, 1), roll(right, -8, 1)

    def arrived(slot, y):
        parts = [jnp.where(has[x, y], yr[slot, rows], 0.0) for x, rows in ((-1, top), (0, mid), (1, low))]
        return jnp.concatenate(parts, axis=0)

    carry = lax.fori_loop(0, 3, halo, (arrived(1, -1), arrived(0, 1)), unroll=True)

    def sweep(old_u, new_u, old_w, new_w):
        def run(i, _):
            (c0, c1), (n0, n1) = stencil_full(old_u, i)
            new_u[i, 0] = KEEP * c0 + u1[i, 0] + a_[i, 0] * n0
            new_u[i, 1] = KEEP * c1 + u1[i, 1] + a_[i, 1] * n1
            (c0, c1), (n0, n1) = stencil_full(old_w, i)
            new_w[i, 0] = KEEP * c0 + a_[i, 0] * n0
            new_w[i, 1] = KEEP * c1 + a_[i, 1] * n1
            return 0
        return run

    def finish(i, _):
        z = source(i - 1)
        weight, s1 = a_[i, 0, OWN], u1[i, 0, OWN]
        c, n = stencil_own(u3, i)
        s4 = s1 + weight * n
        b, n = stencil_own(w2, i)
        w3 = KEEP * b + weight * n
        second = u2[i, 0, OWN]
        total = w0[i, 0, OWN] * s4 + w1[i, 0, OWN] * (c - KEEP * second) + b * (second - KEEP * s1) + w3 * s1
        rg[z] = (2.0 / RELAX) * jnp.exp(-2.0 * lr[z]) * total
        it[z] = jnp.where(ms[z] > 0, KEEP * c + s4, LAND * fo[z])
        return 0

    first = sweep(u1, u2, w0, w1)
    second = sweep(u2, u3, w1, w2)
    first(15, 0)
    ring = ((u1, 16, 2), (w0, 16, 2), (u1, 15, 1), (w0, 15, 1), (a_, 16, 1))
    above, below, columns = None, None, None
    at = 0
    for ref, i, depth in ring:
        t = roll(ref[i, 0, top], -at, 0)
        b = roll(ref[i, 0, low], at, 0)
        above = t if above is None else jnp.where(row8 < 8 - at, t, above)
        below = b if below is None else jnp.where(row8 >= at, b, below)
        at += depth
    for k in range(6):
        part, at = None, 0
        for ref, i, depth in ring:
            c = roll(ref[i, 1, pl.ds(8 * k, 8)], at + depth + 16 * k, 1)
            part = c if part is None else jnp.where(lane8 >= at + 16 * k, c, part)
            at += 2 * depth
        columns = part if columns is None else jnp.where(lane8 >= 16 * k, part, columns)
    gs[first8] = above
    gs[pl.ds(8, 8)] = below
    gs[pl.ds(16, 8)] = columns
    gs[pl.ds(24, 32)] = u2[15, 0, OWN]
    gs[pl.ds(56, 32)] = w1[15, 0, OWN]
    @pl.when((gz == 1) & (turn < 2))
    def _():
        gcopy.start()

    send_layers(2)

    for side in far:
        @pl.when(has[side] & (gz == 1) & (place <= 2))
        def _():
            far[side].start()
    send_layers(3)
    for side in far:
        @pl.when(has[-side[0], -side[1]])
        def _():
            far[side].wait_recv()
    lax.fori_loop(3, 16, halo, carry)
    lax.fori_loop(1, 6, first, 0, unroll=5)
    send_layers(4)
    lax.fori_loop(6, 15, first, 0, unroll=3)

    lax.fori_loop(1, 15, second, 0, unroll=2)
    @pl.when(gz == 0)
    def _():
        pl.semaphore_wait(ready, 1)
        zcopy.start()
        gcopy.start()
    lax.fori_loop(1, 14, finish, 0)

    zcopy.wait_recv()
    for j, (ref, i) in enumerate(((u1, 17), (u1, 18), (w0, 17), (w0, 18), (a_, 17))):
        ref[i, 0, OWN] = zr[j]
    gcopy.wait_recv()
    above, below, columns = gr[first8], gr[pl.ds(8, 8)], gr[pl.ds(16, 8)]
    u2[18, 0, OWN] = gr[pl.ds(24, 32)]
    w1[18, 0, OWN] = gr[pl.ds(56, 32)]
    at = 0
    for ref, i, depth in ring:
        ref[33 - i, 0, top] = roll(above, at, 0)
        ref[33 - i, 0, low] = roll(below, -at, 0)
        at += depth
    for k in range(6):
        at = 0
        for ref, i, depth in ring:
            ref[33 - i, 1, pl.ds(8 * k, 8)] = roll(columns, -(at + depth + 16 * k), 1)
            at += 2 * depth

    lax.fori_loop(16, 18, first, 0, unroll=True)
    lax.fori_loop(15, 18, second, 0, unroll=True)
    lax.fori_loop(14, 17, finish, 0, unroll=True)

    for side in SIDES:
        @pl.when(has[side])
        def _():
            copies[side].wait_send()
    for side in far:
        @pl.when(has[side])
        def _():
            far[side].wait_send()
    zcopy.wait_send()
    gcopy.wait_send()


def solution(mesh):
    sizes = mesh.shape["gx"], mesh.shape["gy"]
    spec = P("gz", "gx", "gy")

    def body(log_range, sea_mask, forcing, cotangent):
        block = log_range.shape
        f32 = jnp.float32
        field = pltpu.VMEM((19, 2, 48, 128), f32)
        return pl.pallas_call(
            functools.partial(kernel, sizes),
            out_shape=[pltpu.VMEM(block, f32)] * 2,
            in_specs=[pl.BlockSpec(memory_space=pltpu.HBM)] * 4,
            out_specs=[pl.BlockSpec(memory_space=pltpu.VMEM)] * 2,
            scratch_shapes=[
                pltpu.VMEM(block, f32), pltpu.VMEM(block, jnp.int32), pltpu.VMEM(block, f32), pltpu.VMEM(block, f32),
                field, field, field, field, field, field, field,
                pltpu.VMEM((2, 16, 8, 128), f32), pltpu.VMEM((2, 16, 8, 128), f32),
                pltpu.VMEM((2, 32, 128), f32), pltpu.VMEM((2, 48, 128), f32),
                pltpu.VMEM((5, 32, 128), f32), pltpu.VMEM((5, 32, 128), f32),
                pltpu.VMEM((88, 128), f32), pltpu.VMEM((88, 128), f32),
                pltpu.SemaphoreType.DMA((4,)), pltpu.SemaphoreType.DMA((2, 12)),
                pltpu.SemaphoreType.REGULAR,
            ],
            compiler_params=pltpu.CompilerParams(collective_id=0, has_side_effects=True, vmem_limit_bytes=48 * 1024 * 1024),
            cost_estimate=pl.CostEstimate(flops=10_000_000, bytes_accessed=1_600_000, transcendentals=200_000),
        )(*(pltpu.with_memory_space_constraint(x, pltpu.HBM) for x in (log_range, sea_mask, forcing, cotangent)))

    def store(it, rg, it_h, rg_h, sem):
        copies = [pltpu.make_async_copy(v.at[pl.ds(16 * h, 16)], o.at[pl.ds(16 * h, 16)], sem.at[i, h])
                  for i, (v, o) in enumerate(((it, it_h), (rg, rg_h))) for h in range(1)]
        for copy in copies:
            copy.start()
        for copy in copies:
            copy.wait()

    def whole(*args):
        parts = body(*args)
        parts = [pltpu.with_memory_space_constraint(x, pltpu.VMEM) for x in parts]
        return pl.pallas_call(store, out_shape=[jax.ShapeDtypeStruct(x.shape, jnp.float32) for x in parts],
                              in_specs=[pl.BlockSpec(memory_space=pltpu.VMEM)] * 2,
                              out_specs=[pl.BlockSpec(memory_space=pl.ANY)] * 2,
                              scratch_shapes=[pltpu.SemaphoreType.DMA((2, 1))])(*parts)

    return jax.shard_map(whole, mesh=mesh, in_specs=(spec,) * 4, out_specs=(spec, spec), check_vma=False)
```
